256 devices in a mesh: row: 8 (over y_hi, x), col: 2 (over y_lo), chan: 16 (over z, core).
Axes of the slice: x: 4, y: 4 (y_hi: 2, y_lo: 2; y = y_hi * 2 + y_lo), z: 8, core: 2. Of those that a mesh axis runs over, the one named last changes fastest.
Arguments:
- visibilities: float32 [2, 64, 2, 1024, 1024], P(None, 'chan', None, 'row', 'col'), parts along dimension 1, as said below
- stations: float32 [2, 16384], P(None, 'chan'), parts along dimension 1, may hold values from -300 to 300
- pixels: int32 [16384], P('chan'), parts along dimension 0, may hold values from 0 to 1048575
- flux: float32 [64, 2, 1024], P('chan'), parts along dimension 0, may hold values from 0.01 to 0.1
- freqs: float32 [64], P('chan'), parts along dimension 0, may hold values from 0.8 to 1.25
- flags: int32 [64, 1024], P('chan'), parts along dimension 0, may hold values 0 or 1
Outputs:
- gains: float32 [2, 64, 2, 1024], P(None, 'chan'), parts along dimension 1
- residual: float32 [2, 64, 2, 1024, 1024], P(None, 'chan', None, 'row', 'col'), parts along dimension 1
The draws below stay inside these ranges and needn't reach their ends.
There are 16 independent parts, one for each index of `chan`. The reference program is written for one: setup_inputs(seed, part) draws one part's arguments, and reference() takes and returns one part's arrays. A program takes and returns all parts, laid end to end along the dimension named above; each array names one. Nothing has to cross between parts.
Inputs may be any that keep to these rules, and one draw needn't show every extreme that they name: For each channel and polarisation the matrix visibilities[0] + i visibilities[1] over the two station dimensions is Hermitian up to float32 rounding.
All inputs are finite; a program needn't handle non-finite values.
Results may differ from the reference program's by a relative error of at most 0.0047.
Values sent between devices are 32-bit elements; how exact they have to be, the bound alone decides.
No kernel may reach another device: no remote copies, remote signals or barrier semaphores. Data moves between devices by JAX's collectives and lax.ppermute only.
A program may use at most 64 MiB of HBM per device.

```python
import math
import jax
import jax.numpy as jnp
from jax import lax

N = 1024
K = 1024
P_SIZE = 2
CH = 4
ITERS = 8
SIDE = 1024


def sky_parts(key):
    first, second, third, fourth = jax.random.split(key, 4)
    positions = jax.random.uniform(first, (2, N), jnp.float32, -300.0, 300.0)
    drawn = jax.random.randint(second, (K,), 0, SIDE * SIDE, dtype=jnp.int32)
    places = jnp.arange(K, dtype=jnp.int32)
    drawn = jnp.where(places == 0, 0, drawn)
    drawn = jnp.where(places == K - 1, SIDE * SIDE - 1, drawn)
    brightness = jnp.exp(jax.random.uniform(third, (CH, P_SIZE, K), jnp.float32, math.log(0.01), math.log(0.1)))
    ratios = jnp.exp(jax.random.uniform(fourth, (CH,), jnp.float32, math.log(0.8), math.log(1.25)))
    return (positions, drawn, brightness, ratios)


def sky_model(positions, drawn, brightness, ratios):
    across = (drawn % SIDE).astype(jnp.float32)
    down = (drawn // SIDE).astype(jnp.float32)
    lvals = (across + 0.5) / SIDE * 0.5 - 0.25
    mvals = (down + 0.5) / SIDE * 0.5 - 0.25
    base = positions[0][:, None] * lvals[None, :] + positions[1][:, None] * mvals[None, :]
    phase = 2.0 * math.pi * ratios[:, None, None] * base[None]
    cosines = jnp.cos(phase)
    sines = jnp.sin(phase)
    cos_weighted = cosines[:, None] * brightness[:, :, None, :]
    sin_weighted = sines[:, None] * brightness[:, :, None, :]
    high = lax.Precision.HIGHEST
    model_re = jnp.einsum('cpnk,cmk->cpnm', cos_weighted, cosines, precision=high) + jnp.einsum('cpnk,cmk->cpnm', sin_weighted, sines, precision=high)
    model_im = jnp.einsum('cpnk,cmk->cpnm', cos_weighted, sines, precision=high) - jnp.einsum('cpnk,cmk->cpnm', sin_weighted, cosines, precision=high)
    return (model_re, model_im)


def draw_stations(key, part):
    return sky_parts(key)[0]


def draw_pixels(key, part):
    return sky_parts(key)[1]


def draw_flux(key, part):
    return sky_parts(key)[2]


def draw_freqs(key, part):
    return sky_parts(key)[3]


def draw_visibilities(key, part):
    positions, drawn, brightness, ratios = sky_parts(key)
    model_re, model_im = sky_model(positions, drawn, brightness, ratios)
    key = jax.random.fold_in(key, 11)
    first, second, third, fourth = jax.random.split(key, 4)
    shape = (CH, P_SIZE, N, N)
    spread = 0.1 * jnp.sqrt(jnp.float32(K) * 0.00215)
    angles = jax.random.uniform(fourth, (CH, P_SIZE, N), jnp.float32, -math.pi, math.pi)
    amplitude = jax.random.uniform(third, (CH, P_SIZE, N), jnp.float32, 0.8, 1.2)
    real_raw = jax.random.truncated_normal(first, -4.0, 4.0, shape, jnp.float32)
    imag_raw = jax.random.truncated_normal(second, -4.0, 4.0, shape, jnp.float32)
    gain_re = amplitude * jnp.cos(angles)
    gain_im = amplitude * jnp.sin(angles)
    gqr = gain_re[:, :, None, :]
    gqi = gain_im[:, :, None, :]
    half_re = model_re * gqr + model_im * gqi
    half_im = model_im * gqr - model_re * gqi
    gpr = gain_re[..., None]
    gpi = gain_im[..., None]
    signal_re = gpr * half_re - gpi * half_im
    signal_im = gpr * half_im + gpi * half_re
    noise_re = (real_raw + jnp.swapaxes(real_raw, 2, 3)) * (0.7071 * spread)
    noise_im = (imag_raw - jnp.swapaxes(imag_raw, 2, 3)) * (0.7071 * spread)
    return jnp.stack([signal_re + noise_re, signal_im + noise_im])


def set_ends(entries, rng, low, high):
    spot = [jax.random.randint(jax.random.fold_in(rng, axis), (), 0, length) for axis, length in enumerate(entries.shape)]
    widest = entries.shape.index(max(entries.shape))
    next_to = spot[:widest] + [(spot[widest] + 1) % entries.shape[widest]] + spot[widest + 1:]
    return entries.at[tuple(spot)].set(low).at[tuple(next_to)].set(high)


def setup_inputs(seed: int = 0, part: int = 0) -> dict:
    key_of = jax.random.split(jax.random.key(seed), 7)
    part_splits = jax.random.split(jax.random.fold_in(key_of[6], part), 7)
    visibilities = draw_visibilities(jax.random.fold_in(jax.random.fold_in(key_of[6], part), 71), part)
    stations = draw_stations(jax.random.fold_in(jax.random.fold_in(key_of[6], part), 71), part)
    pixels = draw_pixels(jax.random.fold_in(jax.random.fold_in(key_of[6], part), 71), part)
    flux = draw_flux(jax.random.fold_in(jax.random.fold_in(key_of[6], part), 71), part)
    freqs = draw_freqs(jax.random.fold_in(jax.random.fold_in(key_of[6], part), 71), part)
    flags = set_ends((jax.random.randint(part_splits[5], (CH, N), 0, 16) < 15).astype(jnp.int32), jax.random.fold_in(part_splits[5], 1), 0, 1)
    return dict(visibilities=visibilities, stations=stations, pixels=pixels, flux=flux, freqs=freqs, flags=flags)


two_pi = 2.0 * math.pi


def directions(pixels):
    across = (pixels % SIDE).astype(jnp.float32)
    down = (pixels // SIDE).astype(jnp.float32)
    lvals = (across + 0.5) / SIDE * 0.5 - 0.25
    mvals = (down + 0.5) / SIDE * 0.5 - 0.25
    return lvals, mvals


def steering(coord_u, coord_v, lvals, mvals, ratio):
    phase = two_pi * ratio * (coord_u[:, None] * lvals[None, :] + coord_v[:, None] * mvals[None, :])
    return jnp.cos(phase), jnp.sin(phase)


def predict(cos_rows, sin_rows, cos_cols, sin_cols, flux_one):
    left = jnp.concatenate([cos_rows[None] * flux_one[:, None, :], sin_rows[None] * flux_one[:, None, :]], -1).astype(jnp.bfloat16)
    right = jnp.concatenate([jnp.concatenate([cos_cols, sin_cols], 1), jnp.concatenate([sin_cols, -cos_cols], 1)], 0).astype(jnp.bfloat16)
    out = jnp.einsum("prk,ck->prc", left.astype(jnp.float32), right.astype(jnp.float32), precision=lax.Precision.HIGHEST)
    width = cos_cols.shape[0]
    return out[..., :width], out[..., width:]


def partial_sums(vis_re, vis_im, m_re, m_im, g_re_q, g_im_q, w_q):
    gre = g_re_q[..., None]
    gim = g_im_q[..., None]
    weight = w_q[:, None, :, None]
    z_re = gre * m_re - gim * m_im
    z_im = gre * m_im + gim * m_re
    num_re = jnp.sum(weight * (vis_re * z_re + vis_im * z_im), axis=2)
    num_im = jnp.sum(weight * (vis_re * z_im - vis_im * z_re), axis=2)
    den = jnp.sum(weight * (z_re * z_re + z_im * z_im), axis=2)
    return num_re, num_im, den


def update(g_re, g_im, num_re, num_im, den, weight, step):
    wide = weight[:, None, :]
    scale = wide / (den + 1.0 - wide)
    new_re = num_re * scale
    new_im = num_im * scale
    if step % 2 == 1:
        return 0.5 * (new_re + g_re), 0.5 * (new_im + g_im)
    return new_re, new_im


def corrected(vis_re, vis_im, m_re, m_im, g_re_p, g_im_p, g_re_q, g_im_q):
    gqr = g_re_q[:, :, None, :]
    gqi = g_im_q[:, :, None, :]
    a_re = m_re * gqr + m_im * gqi
    a_im = m_im * gqr - m_re * gqi
    gpr = g_re_p[..., None]
    gpi = g_im_p[..., None]
    return vis_re - (gpr * a_re - gpi * a_im), vis_im - (gpr * a_im + gpi * a_re)


def reference(visibilities, stations, pixels, flux, freqs, flags):
    lvals, mvals = directions(pixels)
    channels = visibilities.shape[1]
    model_re = []
    model_im = []
    for chan_index in range(channels):
        cos_all, sin_all = steering(stations[0], stations[1], lvals, mvals, freqs[chan_index])
        part_re, part_im = predict(cos_all, sin_all, cos_all, sin_all, flux[chan_index])
        model_re.append(part_re)
        model_im.append(part_im)
    m_re = jnp.stack(model_re)
    m_im = jnp.stack(model_im)
    weight = flags.astype(jnp.float32)
    g_re = jnp.broadcast_to(weight[:, None, :], m_re.shape[:3]).astype(jnp.float32)
    g_im = jnp.zeros(m_re.shape[:3], jnp.float32)
    for step in range(ITERS):
        num_re, num_im, den = partial_sums(visibilities[0], visibilities[1], m_re, m_im, g_re, g_im, weight)
        g_re, g_im = update(g_re, g_im, num_re, num_im, den, weight, step)
    res_re, res_im = corrected(visibilities[0], visibilities[1], m_re, m_im, g_re, g_im, g_re, g_im)
    return jnp.stack([g_re, g_im]), jnp.stack([res_re, res_im])
```

```python
import functools

import jax
import jax.numpy as jnp
from jax import lax
from jax.experimental import pallas as pl
from jax.experimental.pallas import tpu as pltpu
from jax.sharding import PartitionSpec as P

ITERS = 8
SIDE = 1024
T = 128

SIN = (4.442867982256445, -7.307445413087933, 3.5948021037170865, -0.7844036262695797)
COS = (1.4142134965650144, -6.978850988238961, 5.739461170681741, -1.8835629873024078, 0.3106981918128224)
MAGIC = 12582912.0
F32 = jnp.float32
BF16 = jnp.bfloat16
VMEM_LIMIT = 56 * 1024 * 1024


def poly(y, coeffs):
    out = coeffs[-1]
    for c in reversed(coeffs[:-1]):
        out = out * y + c
    return out


def cos_sin(turns):
    r = turns - ((turns + MAGIC) - MAGIC)
    y = r * r
    s = r * poly(y, SIN)
    c = poly(y, COS)
    return 1.0 - s * s, s * c


def lm_rows(pix):
    across = (pix & (SIDE - 1)).astype(F32)
    down = (pix >> 10).astype(F32)
    lv = (across + 0.5) / SIDE * 0.5 - 0.25
    mv = (down + 0.5) / SIDE * 0.5 - 0.25
    return lv, mv


def spread(rows, out_ref):
    for t in range(8):
        out_ref[t * T:(t + 1) * T, :] = jnp.broadcast_to(rows[t:t + 1, :], (T, T)).T


def dot(a, b, dims):
    return lax.dot_general(a, b, (dims, ((), ())), preferred_element_type=F32)


def own_model(freqs, st, pix, flux, out_re, out_im, ub, vb, left, right):
    cp = lax.axis_index("row")
    f = freqs[cp // 2]
    lv, mv = lm_rows(pix[...])
    spread(st[0] * f, ub)
    spread(st[1] * f, vb)
    fx = flux[cp]

    def step(g, _):
        r = pl.multiple_of(g * 16, 16)
        u = ub[pl.ds(r, 16), :]
        v = vb[pl.ds(r, 16), :]
        for k in range(8):
            c, s = cos_sin(u * lv[k:k + 1, :] + v * mv[k:k + 1, :])
            w = fx[k:k + 1, :]
            lo, hi = k * T, (k + 1) * T
            left[pl.ds(r, 16), lo:hi] = (c * w).astype(BF16)
            left[pl.ds(r, 16), 1024 + lo:1024 + hi] = (s * w).astype(BF16)
            cb = c.astype(BF16)
            right[pl.ds(r, 16), lo:hi] = cb
            right[pl.ds(r, 16), 1024 + lo:1024 + hi] = s.astype(BF16)
            right[pl.ds(r, 16), 2048 + lo:2048 + hi] = -cb
        return 0

    lax.fori_loop(0, 64, step, 0)

    def mm(n, _):
        ns = pl.ds(pl.multiple_of(n * 512, 512), 512)
        for m in range(4):
            rows = slice(m * 256, (m + 1) * 256)
            a = left[rows, :]
            out_re[rows, ns] = dot(a, right[ns, 0:2048], ((1,), (1,)))
            out_im[rows, ns] = dot(a, right[ns, 1024:3072], ((1,), (1,)))
        return 0

    lax.fori_loop(0, 2, mm, 0)


def block_model(freqs, st, pix, flux, out_re, out_im, ub, vb, lb, mb, left, right):
    i, j = lax.axis_index("row"), lax.axis_index("col")
    lv, mv = lm_rows(pix[...])
    spread(lv, lb)
    spread(mv, mb)
    ub[...] = jnp.broadcast_to(st[0, pl.ds(i, 1), :], (T, T)).T
    vb[...] = jnp.broadcast_to(st[1, pl.ds(i, 1), :], (T, T)).T

    def chan(ch, _):
        f = freqs[ch]
        f0 = flux[2 * ch]
        f1 = flux[2 * ch + 1]

        def rows(g, _):
            r = pl.multiple_of(g * 16, 16)
            u = ub[pl.ds(r, 16), :] * f
            v = vb[pl.ds(r, 16), :] * f
            for k in range(8):
                c, s = cos_sin(u * lv[k:k + 1, :] + v * mv[k:k + 1, :])
                lo, hi = k * T, (k + 1) * T
                for p, fx in enumerate((f0, f1)):
                    w = fx[k:k + 1, :]
                    rr = pl.multiple_of(r + p * T, 16)
                    left[pl.ds(rr, 16), lo:hi] = (c * w).astype(BF16)
                    left[pl.ds(rr, 16), 1024 + lo:1024 + hi] = (s * w).astype(BF16)
            return 0

        lax.fori_loop(0, 8, rows, 0)

        def cols(g, _):
            r = pl.multiple_of(g * 16, 16)
            lk = lb[pl.ds(r, 16), :]
            mk = mb[pl.ds(r, 16), :]
            for q in range(4):
                u = st[0, pl.ds(4 * j + q, 1), :] * f
                v = st[1, pl.ds(4 * j + q, 1), :] * f
                c, s = cos_sin(lk * u + mk * v)
                cb = c.astype(BF16)
                lanes = slice(q * T, (q + 1) * T)
                right[pl.ds(r, 16), lanes] = cb
                right[pl.ds(pl.multiple_of(r + 1024, 16), 16), lanes] = s.astype(BF16)
                right[pl.ds(pl.multiple_of(r + 2048, 16), 16), lanes] = -cb
            return 0

        lax.fori_loop(0, 64, cols, 0)
        for n in range(2):
            lanes = slice(n * 256, (n + 1) * 256)
            re = dot(left[...], right[0:2048, lanes], ((1,), (0,)))
            im = dot(left[...], right[1024:3072, lanes], ((1,), (0,)))
            for p in range(2):
                out_re[2 * ch + p, :, lanes] = re[p * T:(p + 1) * T]
                out_im[2 * ch + p, :, lanes] = im[p * T:(p + 1) * T]
        return 0

    lax.fori_loop(0, 4, chan, 0)


def pack(vis, out):
    i, j = lax.axis_index("row"), lax.axis_index("col")
    r, half = i % 4, i // 4
    off = jnp.where((half == 1) & (j == 0), 1, 0)

    def block(z, n):
        lane = pl.multiple_of(((r + n) % 4) * T, T)
        return vis[z, 0, :, pl.ds(lane, T)]

    for z in range(2):
        out[0, z, 0:T, :] = block(z, off)
        out[0, z, T:2 * T, :] = block(z, off + 1)

    @pl.when(r < 2)
    def _():
        for z in range(2):
            out[0, z, 2 * T:, :] = block(z, 2)[0:64]

    @pl.when(r >= 2)
    def _():
        for z in range(2):
            turned = block(z, 2).T[64:T]
            out[0, z, 2 * T:, :] = -turned if z else turned


def gain_solve(flags, near, far, m_re, m_im, out, cc, halves, diag):
    cp, j = lax.axis_index("row"), lax.axis_index("col")
    w = flags[pl.ds(cp // 2, 1), :].astype(F32)
    eye = lax.broadcasted_iota(jnp.int32, (T, T), 0) == lax.broadcasted_iota(jnp.int32, (T, T), 1)

    def products(row, col, vr, vi):
        rs = pl.ds(pl.multiple_of(row * T, T), T)
        cs = pl.ds(pl.multiple_of(col * T, T), T)
        mr = m_re[rs, cs]
        mi = m_im[rs, cs]
        return vr * mr + vi * mi, vr * mi - vi * mr, mr * mr + mi * mi

    def put(row, col, parts):
        cs = pl.ds(pl.multiple_of(col * T, T), T)
        for n, part in enumerate(parts):
            cc[pl.ds(pl.multiple_of(n * 1024 + row * T, T), T), cs] = part.astype(BF16)

    def fill(row, col, vr, vi):
        put(row, col, products(row, col, vr, vi))
        put(col, row, products(col, row, vr.T, -vi.T))

    for buf, jj in ((near, j), (far, 1 - j)):
        side = 0 if buf is near else 1

        def diagonal(r, _):
            a = 4 * jj + r
            parts = products(a, a, buf[a, 0, 0:T, :], buf[a, 1, 0:T, :])
            for n, part in enumerate(parts):
                diag[pl.ds(8 * n + a, 1), :] = jnp.sum(jnp.where(eye, part, 0.0), axis=0, keepdims=True)
            put(a, a, [jnp.where(eye, 0.0, part) for part in parts])
            fill(a, 4 * jj + (r + 1) % 4, buf[a, 0, T:2 * T, :], buf[a, 1, T:2 * T, :])
            for z in range(2):
                halves[z, 2 * side + r % 2, pl.ds(pl.multiple_of((r // 2) * 64, 64), 64), :] = buf[a, z, 2 * T:, :]
            return 0

        lax.fori_loop(0, 4, diagonal, 0)

        def across(p, _):
            fill(4 * jj + p, 4 * jj + p + 2, halves[0, 2 * side + p], halves[1, 2 * side + p])
            return 0

        lax.fori_loop(0, 2, across, 0)
        off = jnp.where(jj == 0, 1, 0)

        def outer(r, _):
            a = 4 * (1 - jj) + r
            fill(a, 4 * jj + (r + off) % 4, buf[a, 0, 0:T, :], buf[a, 1, 0:T, :])
            fill(a, 4 * jj + (r + off + 1) % 4, buf[a, 0, T:2 * T, :], buf[a, 1, T:2 * T, :])
            return 0

        lax.fori_loop(0, 4, outer, 0)

    def row_of(n):
        return jnp.concatenate([diag[8 * n + t:8 * n + t + 1, :] for t in range(8)], 1)

    d_re, d_im, d_den = row_of(0), row_of(1), row_of(2)
    sub = lax.broadcasted_iota(jnp.int32, (16, 1024), 0)

    def split(x):
        return x, x - x.astype(BF16).astype(F32)

    def stack(*rows):
        out = jnp.zeros((16, 1024), F32)
        for n, x in rows:
            out = jnp.where(sub == n, x, out)
        return out

    def one(step, carry):
        g_re, g_im = carry
        hr, hr_lo = split(w * g_re)
        hi, hi_lo = split(w * g_im)
        hd, hd_lo = split(w * (g_re * g_re + g_im * g_im))
        left = jnp.concatenate(
            [
                stack((0, hr), (1, hi), (3, hr_lo), (4, hi_lo)),
                stack((0, -hi), (1, hr), (3, -hi_lo), (4, hr_lo)),
                stack((2, hd), (5, hd_lo)),
            ],
            1,
        ).astype(BF16)
        sums = dot(left, cc[...], ((1,), (0,)))
        num_re = sums[0:1] + sums[3:4] + (hr * d_re - hi * d_im)
        num_im = sums[1:2] + sums[4:5] + (hr * d_im + hi * d_re)
        den = sums[2:3] + sums[5:6] + hd * d_den
        scale = w / (den + 1.0 - w)
        n_re = num_re * scale
        n_im = num_im * scale
        odd = (step % 2) == 1
        return (
            jnp.where(odd, 0.5 * (n_re + g_re), n_re),
            jnp.where(odd, 0.5 * (n_im + g_im), n_im),
        )

    g_re, g_im = lax.fori_loop(0, ITERS, one, (w, jnp.zeros((1, 1024), F32)))
    for n in range(out.shape[0]):
        out[n, 0:1, :] = g_re
        out[n, 1:2, :] = g_im


def residual(vis, m_re, m_im, gall, res, gains):
    i, j = lax.axis_index("row"), lax.axis_index("col")
    active = lax.axis_index("chan") % 2
    cp = pl.program_id(0)

    @pl.when(cp == 0)
    def _():
        for n in range(8):
            for z in range(2):
                gains[z, n // 2, n % 2:n % 2 + 1, :] = gall[2 * n + active, z:z + 1, :]

    src = 2 * cp + active

    def lanes_of(z, t):
        return gall[src, z:z + 1, pl.ds(pl.multiple_of(t * T, T), T)]

    gpr = jnp.broadcast_to(lanes_of(0, i), (T, T)).T
    gpi = jnp.broadcast_to(lanes_of(1, i), (T, T)).T
    for q in range(4):
        lanes = slice(q * T, (q + 1) * T)
        gqr = lanes_of(0, 4 * j + q)
        gqi = lanes_of(1, 4 * j + q)
        mr = m_re[0, :, lanes]
        mi = m_im[0, :, lanes]
        ar = mr * gqr + mi * gqi
        ai = mi * gqr - mr * gqi
        res[0, 0, :, lanes] = vis[0, 0, :, lanes] - (gpr * ar - gpi * ai)
        res[1, 0, :, lanes] = vis[1, 0, :, lanes] - (gpr * ai + gpi * ar)


SMEM = pl.BlockSpec(memory_space=pltpu.SMEM)
VMEM = pl.BlockSpec(memory_space=pltpu.VMEM)


def shape(*dims):
    return jax.ShapeDtypeStruct(dims, F32)


def body(rows, cols, chans, visibilities, stations, pixels, flux, freqs, flags):
    vis = visibilities.reshape(2, 8, T, 512)
    st = stations.reshape(2, 8, T)
    pix = pixels.reshape(8, T)
    fx = flux.reshape(8, 8, T)
    params = pltpu.CompilerParams(vmem_limit_bytes=VMEM_LIMIT)

    with jax.named_scope("pack"):
        packed = pl.pallas_call(
            pack,
            grid=(8,),
            out_shape=shape(8, 2, 320, T),
            in_specs=[pl.BlockSpec((2, 1, T, 512), lambda n: (0, n, 0, 0))],
            out_specs=pl.BlockSpec((1, 2, 320, T), lambda n: (n, 0, 0, 0)),
            compiler_params=params,
            cost_estimate=pl.CostEstimate(flops=1 << 20, bytes_accessed=7 << 20, transcendentals=0),
        )(vis)
    with jax.named_scope("to_the_rows"):
        near = lax.all_to_all(packed, "row", 0, 0, tiled=True)

    with jax.named_scope("own_model"):
        m_re, m_im = pl.pallas_call(
            own_model,
            out_shape=(shape(1024, 1024), shape(1024, 1024)),
            in_specs=[SMEM, VMEM, VMEM, VMEM],
            out_specs=(VMEM, VMEM),
            scratch_shapes=[
                pltpu.VMEM((1024, T), F32),
                pltpu.VMEM((1024, T), F32),
                pltpu.VMEM((1024, 2048), BF16),
                pltpu.VMEM((1024, 3072), BF16),
            ],
            compiler_params=params,
            cost_estimate=pl.CostEstimate(flops=8 << 30, bytes_accessed=8 << 20, transcendentals=2 << 20),
        )(freqs, st, pix, fx)
    near, m_re, m_im = lax.optimization_barrier((near, m_re, m_im))

    with jax.named_scope("to_the_active_column"):
        pairs = []
        for z in range(chans):
            for r in range(rows):
                to = z % 2
                pairs.append((((r * cols) + 1 - to) * chans + z, ((r * cols) + to) * chans + z))
        far = lax.ppermute(near, ("row", "col", "chan"), pairs)

    with jax.named_scope("block_model"):
        b_re, b_im = pl.pallas_call(
            block_model,
            out_shape=(shape(8, T, 512), shape(8, T, 512)),
            in_specs=[SMEM, VMEM, VMEM, VMEM],
            out_specs=(VMEM, VMEM),
            scratch_shapes=[
                pltpu.VMEM((T, T), F32),
                pltpu.VMEM((T, T), F32),
                pltpu.VMEM((1024, T), F32),
                pltpu.VMEM((1024, T), F32),
                pltpu.VMEM((256, 2048), BF16),
                pltpu.VMEM((3072, 512), BF16),
            ],
            compiler_params=params,
            cost_estimate=pl.CostEstimate(flops=4 << 30, bytes_accessed=4 << 20, transcendentals=5 << 20),
        )(freqs, st, pix, fx)
    far, b_re, b_im = lax.optimization_barrier((far, b_re, b_im))

    with jax.named_scope("gain_solve"):
        g = pl.pallas_call(
            gain_solve,
            out_shape=shape(rows * cols, 2, 1024),
            in_specs=[VMEM] * 5,
            out_specs=VMEM,
            scratch_shapes=[
                pltpu.VMEM((3072, 1024), BF16),
                pltpu.VMEM((2, 4, T, T), F32),
                pltpu.VMEM((24, T), F32),
            ],
            compiler_params=params,
            cost_estimate=pl.CostEstimate(flops=800 << 20, bytes_accessed=14 << 20, transcendentals=0),
        )(flags, near, far, m_re, m_im)

    with jax.named_scope("gather_gains"):
        gall = lax.all_to_all(g, ("row", "col"), 0, 0, tiled=True)

    with jax.named_scope("residual"):
        res, gains = pl.pallas_call(
            residual,
            grid=(8,),
            out_shape=(shape(2, 8, T, 512), shape(2, 4, 2, 1024)),
            in_specs=[
                pl.BlockSpec((2, 1, T, 512), lambda n: (0, n, 0, 0)),
                pl.BlockSpec((1, T, 512), lambda n: (n, 0, 0)),
                pl.BlockSpec((1, T, 512), lambda n: (n, 0, 0)),
                VMEM,
            ],
            out_specs=(
                pl.BlockSpec((2, 1, T, 512), lambda n: (0, n, 0, 0)),
                pl.BlockSpec((2, 4, 2, 1024), lambda n: (0, 0, 0, 0)),
            ),
            compiler_params=params,
            cost_estimate=pl.CostEstimate(flops=32 << 20, bytes_accessed=12 << 20, transcendentals=0),
        )(vis, b_re, b_im, gall)
    return gains, res.reshape(2, 4, 2, T, 512)


def solution(mesh):
    in_specs = (
        P(None, "chan", None, "row", "col"),
        P(None, "chan"),
        P("chan"),
        P("chan", None, None),
        P("chan"),
        P("chan", None),
    )
    out_specs = (P(None, "chan", None, None), P(None, "chan", None, "row", "col"))
    run = functools.partial(body, mesh.shape["row"], mesh.shape["col"], mesh.shape["chan"])
    return jax.shard_map(run, mesh=mesh, in_specs=in_specs, out_specs=out_specs, check_vma=False)
```

```python
import functools

import jax
import jax.numpy as jnp
from jax import lax
from jax.experimental import pallas as pl
from jax.experimental.pallas import tpu as pltpu
from jax.sharding import PartitionSpec as P

ITERS = 8
SIDE = 1024
T = 128

SIN = (4.442867982256445, -7.307445413087933, 3.5948021037170865, -0.7844036262695797)
COS = (1.4142134965650144, -6.978850988238961, 5.739461170681741, -1.8835629873024078, 0.3106981918128224)
MAGIC = 12582912.0
F32 = jnp.float32
BF16 = jnp.bfloat16
HALF = 160


def poly(y, coeffs):
    out = coeffs[-1]
    for c in reversed(coeffs[:-1]):
        out = out * y + c
    return out


def cos_sin(turns):
    r = turns - ((turns + MAGIC) - MAGIC)
    y = r * r
    s = r * poly(y, SIN)
    c = poly(y, COS)
    return 1.0 - s * s, s * c


def lm_rows(pix):
    across = (pix & (SIDE - 1)).astype(F32)
    down = (pix >> 10).astype(F32)
    lv = (across + 0.5) / SIDE * 0.5 - 0.25
    mv = (down + 0.5) / SIDE * 0.5 - 0.25
    return lv, mv


def spread(rows, out_ref):
    for t in range(8):
        out_ref[t * T:(t + 1) * T, :] = jnp.broadcast_to(rows[t:t + 1, :], (T, T)).T


def dot(a, b, dims):
    return lax.dot_general(a, b, (dims, ((), ())), preferred_element_type=F32)


def own_model(freqs, st, pix, flux, own_re, own_im, ub, vb, left, right, oo, sem):
    i = lax.axis_index("row")

    @pl.when(lax.axis_index("col") == lax.axis_index("chan") % 2)
    def _():
        f = freqs[i // 2]
        lv, mv = lm_rows(pix[...])
        spread(st[0] * f, ub)
        spread(st[1] * f, vb)
        fx = flux[i]

        def waves(g, _):
            r = pl.multiple_of(g * 16, 16)
            u = ub[pl.ds(r, 16), :]
            v = vb[pl.ds(r, 16), :]
            for k in range(8):
                c, s = cos_sin(u * lv[k:k + 1, :] + v * mv[k:k + 1, :])
                w = fx[k:k + 1, :]
                lo, hi = k * T, (k + 1) * T
                left[pl.ds(r, 16), lo:hi] = (c * w).astype(BF16)
                left[pl.ds(r, 16), 1024 + lo:1024 + hi] = (s * w).astype(BF16)
                cb = c.astype(BF16)
                right[pl.ds(r, 16), lo:hi] = cb
                right[pl.ds(r, 16), 1024 + lo:1024 + hi] = s.astype(BF16)
                right[pl.ds(r, 16), 2048 + lo:2048 + hi] = -cb
            return 0

        lax.fori_loop(0, 64, waves, 0)

        def copies(m):
            rs = pl.ds(pl.multiple_of(m * 256, 256), 256)
            return [pltpu.make_async_copy(oo.at[z, rs], (own_re, own_im)[z].at[rs], sem.at[z, m]) for z in range(2)]

        def rows(m, _):
            rs = pl.ds(pl.multiple_of(m * 256, 256), 256)
            for n in range(2):
                cs = slice(n * 512, (n + 1) * 512)
                for z in range(2):
                    oo[z, rs, cs] = dot(left[rs, :], right[cs, z * 1024:z * 1024 + 2048], ((1,), (1,)))
            for copy in copies(m):
                copy.start()
            return 0

        lax.fori_loop(0, 4, rows, 0)
        for m in range(4):
            for copy in copies(m):
                copy.wait()


def block_model(freqs, st, pix, flux, blk_re, blk_im, rub, rvb, lb, mb, left, right, bo, sem):
    i, j = lax.axis_index("row"), lax.axis_index("col")
    lv, mv = lm_rows(pix[...])
    spread(lv, lb)
    spread(mv, mb)
    rub[...] = jnp.broadcast_to(st[0, pl.ds(i, 1), :], (T, T)).T
    rvb[...] = jnp.broadcast_to(st[1, pl.ds(i, 1), :], (T, T)).T

    def copies(ch):
        rs = pl.ds(2 * ch, 2)
        return [pltpu.make_async_copy(bo.at[z, rs], (blk_re, blk_im)[z].at[rs], sem.at[z, ch]) for z in range(2)]

    def chan(ch, _):
        f = freqs[ch]
        fluxes = [flux[2 * ch + p] for p in range(2)]
        us = [st[0, pl.ds(4 * j + q, 1), :] * f for q in range(4)]
        vs = [st[1, pl.ds(4 * j + q, 1), :] * f for q in range(4)]

        def rows(g, _):
            r = pl.multiple_of(g * 16, 16)
            u = rub[pl.ds(r, 16), :] * f
            v = rvb[pl.ds(r, 16), :] * f
            for k in range(8):
                c, s = cos_sin(u * lv[k:k + 1, :] + v * mv[k:k + 1, :])
                lo, hi = k * T, (k + 1) * T
                for p in range(2):
                    w = fluxes[p][k:k + 1, :]
                    rs = pl.ds(pl.multiple_of(r + p * T, 16), 16)
                    left[rs, lo:hi] = (c * w).astype(BF16)
                    left[rs, 1024 + lo:1024 + hi] = (s * w).astype(BF16)
            return 0

        lax.fori_loop(0, 8, rows, 0)

        def cols(g, _):
            r = pl.multiple_of(g * 16, 16)
            lk = lb[pl.ds(r, 16), :]
            mk = mb[pl.ds(r, 16), :]
            for q in range(4):
                c, s = cos_sin(lk * us[q] + mk * vs[q])
                cb = c.astype(BF16)
                lanes = slice(q * T, (q + 1) * T)
                right[pl.ds(r, 16), lanes] = cb
                right[pl.ds(pl.multiple_of(r + 1024, 16), 16), lanes] = s.astype(BF16)
                right[pl.ds(pl.multiple_of(r + 2048, 16), 16), lanes] = -cb
            return 0

        lax.fori_loop(0, 64, cols, 0, unroll=2)
        for n in range(2):
            lanes = slice(n * 256, (n + 1) * 256)
            for z in range(2):
                out = dot(left[...], right[z * 1024:z * 1024 + 2048, lanes], ((1,), (0,)))
                for p in range(2):
                    bo[z, 2 * ch + p, :, lanes] = out[p * T:(p + 1) * T]
        for copy in copies(ch):
            copy.start()
        return 0

    lax.fori_loop(0, 4, chan, 0)
    for ch in range(4):
        for copy in copies(ch):
            copy.wait()


def pack(vis, packed, vin, chunk, in_sem, one_sem, two_sem):
    i, j = lax.axis_index("row"), lax.axis_index("col")
    r, half = i % 4, i // 4
    off = jnp.where((half == 1) & (j == 0), 1, 0)
    turn = jnp.where(j == lax.axis_index("chan") % 2, 0, 4)
    loads = [pltpu.make_async_copy(vis.at[:, k], vin.at[k], in_sem.at[k]) for k in range(8)]
    stores = []
    for k in range(8):
        stores.append(pltpu.make_async_copy(chunk.at[k, :, 0:HALF], packed.at[k, :, 0:HALF], one_sem.at[k]))
        stores.append(pltpu.make_async_copy(chunk.at[k, :, HALF:], packed.at[(k + turn) % 8, :, HALF:], two_sem.at[k]))
    for load in loads:
        load.start()
    for k in range(8):
        loads[k].wait()

        def block(z, n):
            lane = pl.multiple_of(((r + n) % 4) * T, T)
            return vin[k, z, :, pl.ds(lane, T)]

        for z in range(2):
            chunk[k, z, 0:T, :] = block(z, off)
            chunk[k, z, T:2 * T, :] = block(z, off + 1)
            third = block(z, 2)
            turned = third.T[64:T]
            chunk[k, z, 2 * T:, :] = jnp.where(r < 2, third[0:64], -turned if z else turned)
        stores[2 * k].start()
        stores[2 * k + 1].start()
    for store in stores:
        store.wait()


def gain_solve(flags_in, near_in, far1, far2, re_in, im_in, out,
               flags, near, far, m_re, m_im, cc, halves, diag, sem):
    cp, j = lax.axis_index("row"), lax.axis_index("col")
    active = lax.axis_index("chan") % 2

    @pl.when(j == active)
    def _():
        first = [
            pltpu.make_async_copy(flags_in, flags, sem.at[0]),
            pltpu.make_async_copy(near_in, near, sem.at[1]),
            pltpu.make_async_copy(re_in, m_re, sem.at[2]),
            pltpu.make_async_copy(im_in, m_im, sem.at[3]),
        ]
        second = [
            pltpu.make_async_copy(far1, far.at[:, :, 0:HALF], sem.at[4]),
            pltpu.make_async_copy(far2, far.at[:, :, HALF:], sem.at[5]),
        ]
        for copy in first + second:
            copy.start()
        solve(cp, j, flags, near, far, m_re, m_im, out, cc, halves, diag, first, second)

    @pl.when(j != active)
    def _():
        out[...] = jnp.zeros_like(out)


def solve(cp, j, flags, near, far, m_re, m_im, out, cc, halves, diag, first, second):
    eye = lax.broadcasted_iota(jnp.int32, (T, T), 0) == lax.broadcasted_iota(jnp.int32, (T, T), 1)

    def products(row, col, vr, vi):
        rs = pl.ds(pl.multiple_of(row * T, T), T)
        cs = pl.ds(pl.multiple_of(col * T, T), T)
        mr = m_re[rs, cs]
        mi = m_im[rs, cs]
        return vr * mr + vi * mi, vr * mi - vi * mr, mr * mr + mi * mi

    def put(row, col, parts):
        cs = pl.ds(pl.multiple_of(col * T, T), T)
        for n, part in enumerate(parts):
            cc[pl.ds(pl.multiple_of(n * 1024 + row * T, T), T), cs] = part.astype(BF16)

    def fill(row, col, vr, vi):
        put(row, col, products(row, col, vr, vi))
        put(col, row, products(col, row, vr.T, -vi.T))

    for buf, jj in ((near, j), (far, 1 - j)):
        side = 0 if buf is near else 1
        for copy in second if side else first:
            copy.wait()

        def diagonal(r, _):
            a = 4 * jj + r
            parts = products(a, a, buf[a, 0, 0:T, :], buf[a, 1, 0:T, :])
            for n, part in enumerate(parts):
                diag[pl.ds(8 * n + a, 1), :] = jnp.sum(jnp.where(eye, part, 0.0), axis=0, keepdims=True)
            put(a, a, [jnp.where(eye, 0.0, part) for part in parts])
            fill(a, 4 * jj + (r + 1) % 4, buf[a, 0, T:2 * T, :], buf[a, 1, T:2 * T, :])
            for z in range(2):
                halves[z, 2 * side + r % 2, pl.ds(pl.multiple_of((r // 2) * 64, 64), 64), :] = buf[a, z, 2 * T:, :]
            return 0

        lax.fori_loop(0, 4, diagonal, 0)

        def across(p, _):
            fill(4 * jj + p, 4 * jj + p + 2, halves[0, 2 * side + p], halves[1, 2 * side + p])
            return 0

        lax.fori_loop(0, 2, across, 0)
        off = jnp.where(jj == 0, 1, 0)

        def outer(r, _):
            a = 4 * (1 - jj) + r
            fill(a, 4 * jj + (r + off) % 4, buf[a, 0, 0:T, :], buf[a, 1, 0:T, :])
            fill(a, 4 * jj + (r + off + 1) % 4, buf[a, 0, T:2 * T, :], buf[a, 1, T:2 * T, :])
            return 0

        lax.fori_loop(0, 4, outer, 0)

    w = flags[pl.ds(cp // 2, 1), :].astype(F32)

    def row_of(n):
        return jnp.concatenate([diag[8 * n + t:8 * n + t + 1, :] for t in range(8)], 1)

    d_re, d_im, d_den = row_of(0), row_of(1), row_of(2)
    sub = lax.broadcasted_iota(jnp.int32, (16, 1024), 0)

    def split(x):
        return x, x - x.astype(BF16).astype(F32)

    def stack(*rows):
        out = jnp.zeros((16, 1024), F32)
        for n, x in rows:
            out = jnp.where(sub == n, x, out)
        return out

    def one(step, carry):
        g_re, g_im = carry
        hr, hr_lo = split(w * g_re)
        hi, hi_lo = split(w * g_im)
        hd, hd_lo = split(w * (g_re * g_re + g_im * g_im))
        left = jnp.concatenate(
            [
                stack((0, hr), (1, hi), (3, hr_lo), (4, hi_lo)),
                stack((0, -hi), (1, hr), (3, -hi_lo), (4, hr_lo)),
                stack((2, hd), (5, hd_lo)),
            ],
            1,
        ).astype(BF16)
        sums = dot(left, cc[...], ((1,), (0,)))
        num_re = sums[0:1] + sums[3:4] + (hr * d_re - hi * d_im)
        num_im = sums[1:2] + sums[4:5] + (hr * d_im + hi * d_re)
        den = sums[2:3] + sums[5:6] + hd * d_den
        scale = w / (den + 1.0 - w)
        n_re = num_re * scale
        n_im = num_im * scale
        odd = (step % 2) == 1
        return (
            jnp.where(odd, 0.5 * (n_re + g_re), n_re),
            jnp.where(odd, 0.5 * (n_im + g_im), n_im),
        )

    g_re, g_im = lax.fori_loop(0, ITERS, one, (w, jnp.zeros((1, 1024), F32)))
    for n in range(out.shape[0]):
        out[n, 0:1, :] = g_re
        out[n, 1:2, :] = g_im


def residual(vis, m_re, m_im, gall, res, gains, v, mr_all, mi_all, o, v_sem, re_sem, im_sem, out_sem):
    i, j = lax.axis_index("row"), lax.axis_index("col")
    active = lax.axis_index("chan") % 2
    loads = []
    stores = []
    for cp in range(8):
        loads.append(
            [
                pltpu.make_async_copy(vis.at[:, cp], v.at[cp], v_sem.at[cp]),
                pltpu.make_async_copy(m_re.at[cp], mr_all.at[cp], re_sem.at[cp]),
                pltpu.make_async_copy(m_im.at[cp], mi_all.at[cp], im_sem.at[cp]),
            ]
        )
        stores.append(pltpu.make_async_copy(o.at[cp], res.at[:, cp], out_sem.at[cp]))
    for group in loads:
        for copy in group:
            copy.start()
    for n in range(8):
        for z in range(2):
            gains[z, n // 2, n % 2:n % 2 + 1, :] = gall[2 * n + active, z:z + 1, :]
    for cp in range(8):
        for copy in loads[cp]:
            copy.wait()
        src = 2 * cp + active

        def lanes_of(z, t):
            return gall[src, z:z + 1, pl.ds(pl.multiple_of(t * T, T), T)]

        gpr = jnp.broadcast_to(lanes_of(0, i), (T, T)).T
        gpi = jnp.broadcast_to(lanes_of(1, i), (T, T)).T
        for q in range(4):
            lanes = slice(q * T, (q + 1) * T)
            gqr = lanes_of(0, 4 * j + q)
            gqi = lanes_of(1, 4 * j + q)
            mr = mr_all[cp, :, lanes]
            mi = mi_all[cp, :, lanes]
            ar = mr * gqr + mi * gqi
            ai = mi * gqr - mr * gqi
            o[cp, 0, :, lanes] = v[cp, 0, :, lanes] - (gpr * ar - gpi * ai)
            o[cp, 1, :, lanes] = v[cp, 1, :, lanes] - (gpr * ai + gpi * ar)
        stores[cp].start()
    for store in stores:
        store.wait()


SMEM = pl.BlockSpec(memory_space=pltpu.SMEM)
VMEM = pl.BlockSpec(memory_space=pltpu.VMEM)
ANY = pl.BlockSpec(memory_space=pl.ANY)


def vmem(mib):
    return pltpu.CompilerParams(vmem_limit_bytes=mib << 20)


def shape(*dims):
    return jax.ShapeDtypeStruct(dims, F32)


def body(rows, cols, chans, visibilities, stations, pixels, flux, freqs, flags):
    vis = visibilities.reshape(2, 8, T, 512)
    st = stations.reshape(2, 8, T)
    pix = pixels.reshape(8, T)
    fx = flux.reshape(8, 8, T)

    with jax.named_scope("pack"):
        packed = pl.pallas_call(
            pack,
            out_shape=shape(8, 2, 2 * HALF, T),
            in_specs=[ANY],
            out_specs=ANY,
            scratch_shapes=[
                pltpu.VMEM((8, 2, T, 512), F32),
                pltpu.VMEM((8, 2, 2 * HALF, T), F32),
                pltpu.SemaphoreType.DMA((8,)),
                pltpu.SemaphoreType.DMA((8,)),
                pltpu.SemaphoreType.DMA((8,)),
            ],
            compiler_params=vmem(60),
            cost_estimate=pl.CostEstimate(flops=1 << 20, bytes_accessed=7 << 20, transcendentals=0),
        )(vis)
    with jax.named_scope("to_the_rows"):
        near = lax.all_to_all(packed, "row", 0, 0, tiled=True)

    with jax.named_scope("own_model"):
        m_re, m_im = pl.pallas_call(
            own_model,
            out_shape=(shape(1024, 1024),) * 2,
            in_specs=[SMEM, VMEM, VMEM, VMEM],
            out_specs=(ANY,) * 2,
            scratch_shapes=[
                pltpu.VMEM((1024, T), F32),
                pltpu.VMEM((1024, T), F32),
                pltpu.VMEM((1024, 2048), BF16),
                pltpu.VMEM((1024, 3072), BF16),
                pltpu.VMEM((2, 1024, 1024), F32),
                pltpu.SemaphoreType.DMA((2, 4)),
            ],
            compiler_params=vmem(24),
            cost_estimate=pl.CostEstimate(flops=8 << 30, bytes_accessed=8 << 20, transcendentals=8 << 20),
        )(freqs, st, pix, fx)
    with jax.named_scope("to_the_active_column"):
        near, m_re, m_im = lax.optimization_barrier((near, m_re, m_im))
        far = []
        for half, turn in enumerate((0, rows // 2)):
            pairs = []
            for z in range(chans):
                to = z % 2
                for r in range(rows):
                    src = (r * cols + 1 - to) * chans + z
                    dst = ((r + turn) % rows * cols + to) * chans + z
                    pairs.append((src, dst))
            piece = near[:, :, half * HALF:(half + 1) * HALF]
            far.append(lax.ppermute(piece, ("row", "col", "chan"), pairs))
    with jax.named_scope("block_model"):
        b_re, b_im = pl.pallas_call(
            block_model,
            out_shape=(shape(8, T, 512),) * 2,
            in_specs=[SMEM, VMEM, VMEM, VMEM],
            out_specs=(ANY,) * 2,
            scratch_shapes=[
                pltpu.VMEM((T, T), F32),
                pltpu.VMEM((T, T), F32),
                pltpu.VMEM((1024, T), F32),
                pltpu.VMEM((1024, T), F32),
                pltpu.VMEM((256, 2048), BF16),
                pltpu.VMEM((3072, 512), BF16),
                pltpu.VMEM((2, 8, T, 512), F32),
                pltpu.SemaphoreType.DMA((2, 4)),
            ],
            compiler_params=vmem(14),
            cost_estimate=pl.CostEstimate(flops=8 << 30, bytes_accessed=4 << 20, transcendentals=8 << 20),
        )(freqs, st, pix, fx)
    far[0], far[1], b_re, b_im = lax.optimization_barrier((far[0], far[1], b_re, b_im))

    with jax.named_scope("gain_solve"):
        g = pl.pallas_call(
            gain_solve,
            out_shape=shape(rows * cols, 2, 1024),
            in_specs=[ANY] * 6,
            out_specs=VMEM,
            scratch_shapes=[
                pltpu.VMEM((4, 1024), jnp.int32),
                pltpu.VMEM((8, 2, 2 * HALF, T), F32),
                pltpu.VMEM((8, 2, 2 * HALF, T), F32),
                pltpu.VMEM((1024, 1024), F32),
                pltpu.VMEM((1024, 1024), F32),
                pltpu.VMEM((3072, 1024), BF16),
                pltpu.VMEM((2, 4, T, T), F32),
                pltpu.VMEM((24, T), F32),
                pltpu.SemaphoreType.DMA((6,)),
            ],
            compiler_params=vmem(26),
            cost_estimate=pl.CostEstimate(flops=800 << 20, bytes_accessed=14 << 20, transcendentals=0),
        )(flags, near, *far, m_re, m_im)

    with jax.named_scope("gather_gains"):
        gall = lax.all_to_all(g, ("row", "col"), 0, 0, tiled=True)

    with jax.named_scope("residual"):
        res, gains = pl.pallas_call(
            residual,
            out_shape=(shape(2, 8, T, 512), shape(2, 4, 2, 1024)),
            in_specs=[ANY, ANY, ANY, VMEM],
            out_specs=(ANY, VMEM),
            scratch_shapes=[
                pltpu.VMEM((8, 2, T, 512), F32),
                pltpu.VMEM((8, T, 512), F32),
                pltpu.VMEM((8, T, 512), F32),
                pltpu.VMEM((8, 2, T, 512), F32),
            ]
            + [pltpu.SemaphoreType.DMA((8,))] * 4,
            compiler_params=vmem(18),
            cost_estimate=pl.CostEstimate(flops=32 << 20, bytes_accessed=12 << 20, transcendentals=0),
        )(vis, b_re, b_im, gall)
    return gains, res.reshape(2, 4, 2, T, 512)


def solution(mesh):
    in_specs = (
        P(None, "chan", None, "row", "col"),
        P(None, "chan"),
        P("chan"),
        P("chan", None, None),
        P("chan"),
        P("chan", None),
    )
    out_specs = (P(None, "chan", None, None), P(None, "chan", None, "row", "col"))
    run = functools.partial(body, mesh.shape["row"], mesh.shape["col"], mesh.shape["chan"])
    return jax.shard_map(run, mesh=mesh, in_specs=in_specs, out_specs=out_specs, check_vma=False)
```

```python
import functools

import jax
import jax.numpy as jnp
from jax import lax
from jax.experimental import pallas as pl
from jax.experimental.pallas import tpu as pltpu
from jax.sharding import PartitionSpec as P

ITERS = 8
SIDE = 1024
T = 128

SIN = (4.442867982256445, -7.307445413087933, 3.5948021037170865, -0.7844036262695797)
COS = (1.4142040804669562, -6.977642056688731, 5.715238393830307, -1.728348659759922)
MAGIC = 12582912.0
F32 = jnp.float32
BF16 = jnp.bfloat16
ROWS = 288


def poly(y, coeffs):
    out = coeffs[-1]
    for c in reversed(coeffs[:-1]):
        out = out * y + c
    return out


def cos_sin(turns):
    r = turns - ((turns + MAGIC) - MAGIC)
    y = r * r
    s = r * poly(y, SIN)
    c = poly(y, COS)
    return 1.0 - s * s, s * c


def lm_rows(pix):
    across = (pix & (SIDE - 1)).astype(F32)
    down = (pix >> 10).astype(F32)
    lv = (across + 0.5) / SIDE * 0.5 - 0.25
    mv = (down + 0.5) / SIDE * 0.5 - 0.25
    return lv, mv


def spread(rows, out_ref):
    for t in range(8):
        out_ref[t * T:(t + 1) * T, :] = jnp.broadcast_to(rows[t:t + 1, :], (T, T)).T


def dot(a, b, dims):
    return lax.dot_general(a, b, (dims, ((), ())), preferred_element_type=F32)


def own_model(freqs, st, pix, flux, own_re, own_im, ub, vb, left, right, oo, sem):
    i = lax.axis_index("row")

    @pl.when(lax.axis_index("col") == lax.axis_index("chan") % 2)
    def _():
        f = freqs[i // 2]
        lv, mv = lm_rows(pix[...])
        spread(st[0] * f, ub)
        spread(st[1] * f, vb)
        fx = flux[i]

        def waves(g, _):
            r = pl.multiple_of(g * 16, 16)
            u = ub[pl.ds(r, 16), :]
            v = vb[pl.ds(r, 16), :]
            for k in range(8):
                c, s = cos_sin(u * lv[k:k + 1, :] + v * mv[k:k + 1, :])
                w = fx[k:k + 1, :]
                lo, hi = k * T, (k + 1) * T
                left[pl.ds(r, 16), lo:hi] = (c * w).astype(BF16)
                left[pl.ds(r, 16), 1024 + lo:1024 + hi] = (s * w).astype(BF16)
                cb = c.astype(BF16)
                right[pl.ds(r, 16), lo:hi] = cb
                right[pl.ds(r, 16), 1024 + lo:1024 + hi] = s.astype(BF16)
                right[pl.ds(r, 16), 2048 + lo:2048 + hi] = -cb
            return 0

        lax.fori_loop(0, 64, waves, 0)

        def copies(m):
            rs = pl.ds(pl.multiple_of(m * 256, 256), 256)
            return [pltpu.make_async_copy(oo.at[z, rs], (own_re, own_im)[z].at[rs], sem.at[z, m]) for z in range(2)]

        def rows(m, _):
            rs = pl.ds(pl.multiple_of(m * 256, 256), 256)
            for n in range(2):
                cs = slice(n * 512, (n + 1) * 512)
                for z in range(2):
                    oo[z, rs, cs] = dot(left[rs, :], right[cs, z * 1024:z * 1024 + 2048], ((1,), (1,)))
            for copy in copies(m):
                copy.start()
            return 0

        lax.fori_loop(0, 4, rows, 0)
        for m in range(4):
            for copy in copies(m):
                copy.wait()


def block_model(first, freqs, st, pix, flux, blk_re, blk_im, rub, rvb, lb, mb, left, right, bo, sem):
    i, j = lax.axis_index("row"), lax.axis_index("col")
    lv, mv = lm_rows(pix[...])
    spread(lv, lb)
    spread(mv, mb)
    rub[...] = jnp.broadcast_to(st[0, pl.ds(i, 1), :], (T, T)).T
    rvb[...] = jnp.broadcast_to(st[1, pl.ds(i, 1), :], (T, T)).T

    def copies(ch):
        rs = pl.ds(2 * ch, 2)
        return [pltpu.make_async_copy(bo.at[z, rs], (blk_re, blk_im)[z].at[rs], sem.at[z, ch]) for z in range(2)]

    def chan(ch, _):
        f = freqs[first + ch]
        fluxes = [flux[2 * (first + ch) + p] for p in range(2)]
        us = [st[0, pl.ds(4 * j + q, 1), :] * f for q in range(4)]
        vs = [st[1, pl.ds(4 * j + q, 1), :] * f for q in range(4)]

        def rows(g, _):
            r = pl.multiple_of(g * 16, 16)
            u = rub[pl.ds(r, 16), :] * f
            v = rvb[pl.ds(r, 16), :] * f
            for k in range(8):
                c, s = cos_sin(u * lv[k:k + 1, :] + v * mv[k:k + 1, :])
                lo, hi = k * T, (k + 1) * T
                for p in range(2):
                    w = fluxes[p][k:k + 1, :]
                    rs = pl.ds(pl.multiple_of(r + p * T, 16), 16)
                    sw = (s * w).astype(BF16)
                    left[rs, lo:hi] = -sw
                    left[rs, 1024 + lo:1024 + hi] = (c * w).astype(BF16)
                    left[rs, 2048 + lo:2048 + hi] = sw
            return 0

        lax.fori_loop(0, 8, rows, 0)

        def cols(g, _):
            r = pl.multiple_of(g * 16, 16)
            lk = lb[pl.ds(r, 16), :]
            mk = mb[pl.ds(r, 16), :]
            for q in range(4):
                c, s = cos_sin(lk * us[q] + mk * vs[q])
                lanes = slice(q * T, (q + 1) * T)
                right[pl.ds(r, 16), lanes] = c.astype(BF16)
                right[pl.ds(pl.multiple_of(r + 1024, 16), 16), lanes] = s.astype(BF16)
            return 0

        lax.fori_loop(0, 64, cols, 0, unroll=2)
        for n in range(2):
            lanes = slice(n * 256, (n + 1) * 256)
            for z in range(2):
                out = dot(left[:, (1 - z) * 1024:(1 - z) * 1024 + 2048], right[:, lanes], ((1,), (0,)))
                for p in range(2):
                    bo[z, 2 * ch + p, :, lanes] = out[p * T:(p + 1) * T]
        for copy in copies(ch):
            copy.start()
        return 0

    lax.fori_loop(0, 2, chan, 0)
    for ch in range(2):
        for copy in copies(ch):
            copy.wait()


DIAGONAL, SOLVING, PASSING = range(3)


def pack(vis, packed, vin, chunk, in_sem, one_sem, two_sem):
    i, j = lax.axis_index("row"), lax.axis_index("col")
    r, half = i % 4, i // 4
    solving = j == lax.axis_index("chan") % 2
    turn = jnp.where(solving, 0, 4)
    loads = [pltpu.make_async_copy(vis.at[:, k], vin.at[k], in_sem.at[k]) for k in range(8)]
    stores = []
    for k in range(8):
        stores.append(pltpu.make_async_copy(chunk.at[k, :, 0:T], packed.at[k, :, 0:T], one_sem.at[k]))
        stores.append(
            pltpu.make_async_copy(chunk.at[k, :, T:], packed.at[(k + turn) % 8, :, T:], two_sem.at[k])
        )
    for load in loads:
        load.start()
    left = lax.broadcasted_iota(jnp.int32, (32, T), 1) < 64

    def run(place):
        for k in range(8):
            loads[k].wait()

            def block(z, n):
                lane = pl.multiple_of(((r + n) % 4) * T, T)
                return vin[k, z, :, pl.ds(lane, T)]

            for z in range(2):
                if place == DIAGONAL:
                    chunk[k, z, 0:T, :] = block(z, 1)
                    third = block(z, 2)
                    turned = third.T[64:T]
                    chunk[k, z, T:T + 64, :] = jnp.where(r < 2, third[0:64], -turned if z else turned)
                    own = block(z, 0)
                    chunk[k, z, T + 64:2 * T, :] = own[0:64]
                    chunk[k, z, 2 * T:, :] = jnp.where(left, pltpu.roll(own[64:96], 64, 1), own[96:T])
                else:
                    off = jnp.where(half == 1, 1, 0)
                    chunk[k, z, 0:T, :] = block(z, off)
                    second = block(z, off + 1)
                    if place == SOLVING:
                        chunk[k, z, T:2 * T, :] = second
                        chunk[k, z, 2 * T:, :] = block(z, off + 2)[0:32]
                    else:
                        turned = second.T[32:T]
                        chunk[k, z, T:T + 96, :] = -turned if z else turned
                        chunk[k, z, T + 96:, :] = jnp.zeros((64, T), F32)
            stores[2 * k].start()
            stores[2 * k + 1].start()

    @pl.when(half == j)
    def _():
        run(DIAGONAL)

    @pl.when((half != j) & solving)
    def _():
        run(SOLVING)

    @pl.when((half != j) & jnp.logical_not(solving))
    def _():
        run(PASSING)

    for store in stores:
        store.wait()


def gain_solve(flags, near, far1, far2, m_re, m_im, out, cc, halves, diag):
    cp, j = lax.axis_index("row"), lax.axis_index("col")
    active = lax.axis_index("chan") % 2

    @pl.when(j == active)
    def _():
        solve(cp, j, flags, near, far1, far2, m_re, m_im, out, cc, halves, diag)

    @pl.when(j != active)
    def _():
        out[...] = jnp.zeros_like(out)


def solve(cp, j, flags, near, far1, far2, m_re, m_im, out, cc, halves, diag):

    def of_near(diagonal, a, z, lo, hi):
        return near[a, z, lo:hi, :]

    def of_far(diagonal, a, z, lo, hi):
        if hi <= T:
            return far1[a, z, lo:hi, :]
        start = lo - T + (0 if diagonal else ROWS - T)
        return far2[a % 4, z, start:start + hi - lo, :]
    low = lax.broadcasted_iota(jnp.int32, (64, T), 1) < 64
    eye = lax.broadcasted_iota(jnp.int32, (T, T), 0) == lax.broadcasted_iota(jnp.int32, (T, T), 1)

    def products(row, col, vr, vi):
        rs = pl.ds(pl.multiple_of(row * T, T), T)
        cs = pl.ds(pl.multiple_of(col * T, T), T)
        mr = m_re[rs, cs]
        mi = m_im[rs, cs]
        return vr * mr + vi * mi, vr * mi - vi * mr, mr * mr + mi * mi

    def put(row, col, parts):
        cs = pl.ds(pl.multiple_of(col * T, T), T)
        for n, part in enumerate(parts):
            cc[pl.ds(pl.multiple_of(n * 1024 + row * T, T), T), cs] = part.astype(BF16)

    def fill(row, col, vr, vi):
        put(row, col, products(row, col, vr, vi))
        put(col, row, products(col, row, vr.T, -vi.T))

    for side, (part_of, jj) in enumerate(((of_near, j), (of_far, 1 - j))):
        off = jnp.where(jj == 0, 1, 0)

        def own_block(a, z):
            top = part_of(True, a, z, T + 64, 2 * T)
            turned = jnp.concatenate([top, top], 0).T[64:T]
            last = part_of(True, a, z, 2 * T, ROWS)
            right = jnp.concatenate([pltpu.roll(last, 64, 1), last], 0)
            return jnp.concatenate([top, jnp.where(low, -turned if z else turned, right)], 0)

        def sources(r, _):
            a = 4 * jj + r
            parts = products(a, a, own_block(a, 0), own_block(a, 1))
            for n, part in enumerate(parts):
                diag[pl.ds(8 * n + a, 1), :] = jnp.sum(jnp.where(eye, part, 0.0), axis=0, keepdims=True)
            put(a, a, [jnp.where(eye, 0.0, part) for part in parts])
            fill(a, 4 * jj + (r + 1) % 4, part_of(True, a, 0, 0, T), part_of(True, a, 1, 0, T))
            for z in range(2):
                rs = pl.ds(pl.multiple_of((r // 2) * 64, 64), 64)
                halves[z, 2 * side + r % 2, rs, :] = part_of(True, a, z, T, T + 64)
            b = 4 * (1 - jj) + r
            fill(b, 4 * jj + (r + off) % 4, part_of(False, b, 0, 0, T), part_of(False, b, 1, 0, T))
            if side == 0:
                fill(b, 4 * jj + (r + off + 1) % 4, part_of(False, b, 0, T, 2 * T), part_of(False, b, 1, T, 2 * T))
                for z in range(2):
                    halves[z, 4 + r, 0:32, :] = part_of(False, b, z, 2 * T, ROWS)
            else:
                for z in range(2):
                    halves[z, 4 + (r + off + 1) % 4, 32:T, :] = part_of(False, b, z, T, T + 96)
            return 0

        lax.fori_loop(0, 4, sources, 0)

        def across(p, _):
            fill(4 * jj + p, 4 * jj + p + 2, halves[0, 2 * side + p], halves[1, 2 * side + p])
            return 0

        lax.fori_loop(0, 2, across, 0)

    near_off = jnp.where(j == 0, 1, 0)

    def thirds(r, _):
        fill(4 * (1 - j) + r, 4 * j + (r + near_off + 2) % 4, halves[0, 4 + r], halves[1, 4 + r])
        return 0

    lax.fori_loop(0, 4, thirds, 0)

    w = flags[pl.ds(cp // 2, 1), :].astype(F32)

    def row_of(n):
        return jnp.concatenate([diag[8 * n + t:8 * n + t + 1, :] for t in range(8)], 1)

    d_re, d_im, d_den = row_of(0), row_of(1), row_of(2)
    sub = lax.broadcasted_iota(jnp.int32, (16, 1024), 0)

    def split(x):
        return x, x - x.astype(BF16).astype(F32)

    def stack(*rows):
        out = jnp.zeros((16, 1024), F32)
        for n, x in rows:
            out = jnp.where(sub == n, x, out)
        return out

    def one(step, carry):
        g_re, g_im = carry
        hr, hr_lo = split(w * g_re)
        hi, hi_lo = split(w * g_im)
        hd, hd_lo = split(w * (g_re * g_re + g_im * g_im))
        left = jnp.concatenate(
            [
                stack((0, hr), (1, hi), (3, hr_lo), (4, hi_lo)),
                stack((0, -hi), (1, hr), (3, -hi_lo), (4, hr_lo)),
                stack((2, hd), (5, hd_lo)),
            ],
            1,
        ).astype(BF16)
        sums = dot(left, cc[...], ((1,), (0,)))
        num_re = sums[0:1] + sums[3:4] + (hr * d_re - hi * d_im)
        num_im = sums[1:2] + sums[4:5] + (hr * d_im + hi * d_re)
        den = sums[2:3] + sums[5:6] + hd * d_den
        scale = w / (den + 1.0 - w)
        n_re = num_re * scale
        n_im = num_im * scale
        odd = (step % 2) == 1
        return (
            jnp.where(odd, 0.5 * (n_re + g_re), n_re),
            jnp.where(odd, 0.5 * (n_im + g_im), n_im),
        )

    g_re, g_im = lax.fori_loop(0, ITERS, one, (w, jnp.zeros((1, 1024), F32)))
    for n in range(out.shape[0]):
        out[n, 0:1, :] = g_re
        out[n, 1:2, :] = g_im


def residual(vis, re_early, im_early, re_late, im_late, gall, res, gains, o, out_sem):
    i, j = lax.axis_index("row"), lax.axis_index("col")
    active = lax.axis_index("chan") % 2
    stores = [pltpu.make_async_copy(o.at[cp], res.at[:, cp], out_sem.at[cp]) for cp in range(8)]
    for n in range(8):
        for z in range(2):
            gains[z, n // 2, n % 2:n % 2 + 1, :] = gall[2 * n + active, z:z + 1, :]
    for cp in range(8):
        m_re, m_im = (re_early, im_early) if cp < 4 else (re_late, im_late)
        src = 2 * cp + active

        def lanes_of(z, t):
            return gall[src, z:z + 1, pl.ds(pl.multiple_of(t * T, T), T)]

        gpr = jnp.broadcast_to(lanes_of(0, i), (T, T)).T
        gpi = jnp.broadcast_to(lanes_of(1, i), (T, T)).T
        for q in range(4):
            lanes = slice(q * T, (q + 1) * T)
            gqr = lanes_of(0, 4 * j + q)
            gqi = lanes_of(1, 4 * j + q)
            mr = m_re[cp % 4, :, lanes]
            mi = m_im[cp % 4, :, lanes]
            ar = mr * gqr + mi * gqi
            ai = mi * gqr - mr * gqi
            o[cp, 0, :, lanes] = vis[0, cp, :, lanes] - (gpr * ar - gpi * ai)
            o[cp, 1, :, lanes] = vis[1, cp, :, lanes] - (gpr * ai + gpi * ar)
        stores[cp].start()
    for store in stores:
        store.wait()


SMEM = pl.BlockSpec(memory_space=pltpu.SMEM)
VMEM = pl.BlockSpec(memory_space=pltpu.VMEM)
ANY = pl.BlockSpec(memory_space=pl.ANY)


def vmem(mib):
    return pltpu.CompilerParams(vmem_limit_bytes=mib << 20)


def shape(*dims):
    return jax.ShapeDtypeStruct(dims, F32)


def body(rows, cols, chans, visibilities, stations, pixels, flux, freqs, flags):
    vis = visibilities.reshape(2, 8, T, 512)
    st = stations.reshape(2, 8, T)
    pix = pixels.reshape(8, T)
    fx = flux.reshape(8, 8, T)

    with jax.named_scope("pack"):
        packed = pl.pallas_call(
            pack,
            out_shape=shape(8, 2, ROWS, T),
            in_specs=[ANY],
            out_specs=ANY,
            scratch_shapes=[
                pltpu.VMEM((8, 2, T, 512), F32),
                pltpu.VMEM((8, 2, ROWS, T), F32),
                pltpu.SemaphoreType.DMA((8,)),
                pltpu.SemaphoreType.DMA((8,)),
                pltpu.SemaphoreType.DMA((8,)),
            ],
            compiler_params=vmem(60),
            cost_estimate=pl.CostEstimate(flops=1 << 20, bytes_accessed=7 << 20, transcendentals=0),
        )(vis)
    with jax.named_scope("to_the_rows"):
        near = lax.all_to_all(packed, "row", 0, 0, tiled=True)

    with jax.named_scope("own_model"):
        m_re, m_im = pl.pallas_call(
            own_model,
            out_shape=(shape(1024, 1024),) * 2,
            in_specs=[SMEM, VMEM, VMEM, VMEM],
            out_specs=(ANY,) * 2,
            scratch_shapes=[
                pltpu.VMEM((1024, T), F32),
                pltpu.VMEM((1024, T), F32),
                pltpu.VMEM((1024, 2048), BF16),
                pltpu.VMEM((1024, 3072), BF16),
                pltpu.VMEM((2, 1024, 1024), F32),
                pltpu.SemaphoreType.DMA((2, 4)),
            ],
            compiler_params=vmem(60),
            cost_estimate=pl.CostEstimate(flops=8 << 30, bytes_accessed=8 << 20, transcendentals=8 << 20),
        )(freqs, st, pix, fx)
    def block(first):
        return pl.pallas_call(
            functools.partial(block_model, first),
            out_shape=(shape(4, T, 512),) * 2,
            in_specs=[SMEM, VMEM, VMEM, VMEM],
            out_specs=(ANY,) * 2,
            scratch_shapes=[
                pltpu.VMEM((T, T), F32),
                pltpu.VMEM((T, T), F32),
                pltpu.VMEM((1024, T), F32),
                pltpu.VMEM((1024, T), F32),
                pltpu.VMEM((256, 3072), BF16),
                pltpu.VMEM((2048, 512), BF16),
                pltpu.VMEM((2, 4, T, 512), F32),
                pltpu.SemaphoreType.DMA((2, 2)),
            ],
            compiler_params=vmem(14),
            cost_estimate=pl.CostEstimate(flops=4 << 30, bytes_accessed=2 << 20, transcendentals=4 << 20),
        )(freqs, st, pix, fx)

    with jax.named_scope("to_the_active_column"):
        near, m_re, m_im, *early = lax.optimization_barrier((near, m_re, m_im, *block(0)))
        mine = 4 * lax.axis_index("col")
        pieces = [
            near[:, :, 0:T],
            jnp.concatenate(
                [
                    lax.dynamic_slice_in_dim(near, mine, 4)[:, :, T:ROWS],
                    lax.dynamic_slice_in_dim(near, 4 - mine, 4)[:, :, T:T + 96],
                ],
                2,
            ),
        ]
        far = []
        for piece, turn in zip(pieces, (0, rows // 2)):
            pairs = []
            for z in range(chans):
                to = z % 2
                for r in range(rows):
                    src = (r * cols + 1 - to) * chans + z
                    dst = ((r + turn) % rows * cols + to) * chans + z
                    pairs.append((src, dst))
            far.append(lax.ppermute(piece, ("row", "col", "chan"), pairs))

    with jax.named_scope("block_model"):
        late = block(2)
    far[0], far[1], *late = lax.optimization_barrier((far[0], far[1], *late))

    with jax.named_scope("gain_solve"):
        g = pl.pallas_call(
            gain_solve,
            out_shape=shape(rows * cols, 2, 1024),
            in_specs=[VMEM] * 6,
            out_specs=VMEM,
            scratch_shapes=[
                pltpu.VMEM((3072, 1024), BF16),
                pltpu.VMEM((2, 8, T, T), F32),
                pltpu.VMEM((24, T), F32),
            ],
            compiler_params=vmem(26),
            cost_estimate=pl.CostEstimate(flops=800 << 20, bytes_accessed=14 << 20, transcendentals=0),
        )(flags, near, *far, m_re, m_im)

    with jax.named_scope("gather_gains"):
        gall = lax.all_to_all(g, ("row", "col"), 0, 0, tiled=True)

    with jax.named_scope("residual"):
        res, gains = pl.pallas_call(
            residual,
            out_shape=(shape(2, 8, T, 512), shape(2, 4, 2, 1024)),
            in_specs=[VMEM] * 6,
            out_specs=(ANY, VMEM),
            scratch_shapes=[pltpu.VMEM((8, 2, T, 512), F32), pltpu.SemaphoreType.DMA((8,))],
            compiler_params=vmem(18),
            cost_estimate=pl.CostEstimate(flops=32 << 20, bytes_accessed=12 << 20, transcendentals=0),
        )(vis, *early, *late, gall)
    return gains, res.reshape(2, 4, 2, T, 512)


def solution(mesh):
    in_specs = (
        P(None, "chan", None, "row", "col"),
        P(None, "chan"),
        P("chan"),
        P("chan", None, None),
        P("chan"),
        P("chan", None),
    )
    out_specs = (P(None, "chan", None, None), P(None, "chan", None, "row", "col"))
    run = functools.partial(body, mesh.shape["row"], mesh.shape["col"], mesh.shape["chan"])
    return jax.shard_map(run, mesh=mesh, in_specs=in_specs, out_specs=out_specs, check_vma=False)
```

```python
import functools

import jax
import jax.numpy as jnp
from jax import lax
from jax.experimental import pallas as pl
from jax.experimental.pallas import tpu as pltpu
from jax.sharding import PartitionSpec as P

ITERS = 8
SIDE = 1024
T = 128

SIN = (4.442867982256445, -7.307445413087933, 3.5948021037170865, -0.7844036262695797)
COS = (1.4142040804669562, -6.977642056688731, 5.715238393830307, -1.728348659759922)
MAGIC = 12582912.0
F32 = jnp.float32
BF16 = jnp.bfloat16
ROWS = 288


def poly(y, coeffs):
    out = coeffs[-1]
    for c in reversed(coeffs[:-1]):
        out = out * y + c
    return out


def cos_sin(turns):
    r = turns - ((turns + MAGIC) - MAGIC)
    y = r * r
    s = r * poly(y, SIN)
    c = poly(y, COS)
    return 1.0 - s * s, s * c


def lm_rows(pix):
    across = (pix & (SIDE - 1)).astype(F32)
    down = (pix >> 10).astype(F32)
    lv = (across + 0.5) / SIDE * 0.5 - 0.25
    mv = (down + 0.5) / SIDE * 0.5 - 0.25
    return lv, mv


def spread(rows, out_ref):
    for t in range(8):
        out_ref[t * T:(t + 1) * T, :] = jnp.broadcast_to(rows[t:t + 1, :], (T, T)).T


def dot(a, b, dims):
    return lax.dot_general(a, b, (dims, ((), ())), preferred_element_type=F32)


def own_model(freqs, st, pix, flux, own_re, own_im, ub, vb, left, right, oo, sem):
    i = lax.axis_index("row")

    @pl.when(lax.axis_index("col") == lax.axis_index("chan") % 2)
    def _():
        f = freqs[i // 2]
        lv, mv = lm_rows(pix[...])
        spread(st[0] * f, ub)
        spread(st[1] * f, vb)
        fx = flux[i]

        def waves(g, _):
            r = pl.multiple_of(g * 16, 16)
            u = ub[pl.ds(r, 16), :]
            v = vb[pl.ds(r, 16), :]
            for k in range(8):
                c, s = cos_sin(u * lv[k:k + 1, :] + v * mv[k:k + 1, :])
                w = fx[k:k + 1, :]
                lo, hi = k * T, (k + 1) * T
                left[pl.ds(r, 16), lo:hi] = (c * w).astype(BF16)
                left[pl.ds(r, 16), 1024 + lo:1024 + hi] = (s * w).astype(BF16)
                cb = c.astype(BF16)
                right[pl.ds(r, 16), lo:hi] = cb
                right[pl.ds(r, 16), 1024 + lo:1024 + hi] = s.astype(BF16)
                right[pl.ds(r, 16), 2048 + lo:2048 + hi] = -cb
            return 0

        lax.fori_loop(0, 64, waves, 0)

        def copies(m):
            rs = pl.ds(pl.multiple_of(m * 256, 256), 256)
            return [pltpu.make_async_copy(oo.at[z, rs], (own_re, own_im)[z].at[rs], sem.at[z, m]) for z in range(2)]

        def rows(m, _):
            rs = pl.ds(pl.multiple_of(m * 256, 256), 256)
            for n in range(2):
                cs = slice(n * 512, (n + 1) * 512)
                for z in range(2):
                    oo[z, rs, cs] = dot(left[rs, :], right[cs, z * 1024:z * 1024 + 2048], ((1,), (1,)))
            for copy in copies(m):
                copy.start()
            return 0

        lax.fori_loop(0, 4, rows, 0)
        for m in range(4):
            for copy in copies(m):
                copy.wait()


def block_model(first, freqs, st, pix, flux, blk_re, blk_im, rub, rvb, lb, mb, left, right, bo, sem):
    i, j = lax.axis_index("row"), lax.axis_index("col")
    lv, mv = lm_rows(pix[...])
    spread(lv, lb)
    spread(mv, mb)
    rub[...] = jnp.broadcast_to(st[0, pl.ds(i, 1), :], (T, T)).T
    rvb[...] = jnp.broadcast_to(st[1, pl.ds(i, 1), :], (T, T)).T

    def copies(ch):
        rs = pl.ds(2 * ch, 2)
        return [pltpu.make_async_copy(bo.at[z, rs], (blk_re, blk_im)[z].at[rs], sem.at[z, ch]) for z in range(2)]

    def chan(ch, _):
        f = freqs[first + ch]
        fluxes = [flux[2 * (first + ch) + p] for p in range(2)]
        us = [st[0, pl.ds(4 * j + q, 1), :] * f for q in range(4)]
        vs = [st[1, pl.ds(4 * j + q, 1), :] * f for q in range(4)]

        def rows(g, _):
            r = pl.multiple_of(g * 16, 16)
            u = rub[pl.ds(r, 16), :] * f
            v = rvb[pl.ds(r, 16), :] * f
            for k in range(8):
                c, s = cos_sin(u * lv[k:k + 1, :] + v * mv[k:k + 1, :])
                lo, hi = k * T, (k + 1) * T
                for p in range(2):
                    w = fluxes[p][k:k + 1, :]
                    rs = pl.ds(pl.multiple_of(r + p * T, 16), 16)
                    sw = (s * w).astype(BF16)
                    left[rs, lo:hi] = -sw
                    left[rs, 1024 + lo:1024 + hi] = (c * w).astype(BF16)
                    left[rs, 2048 + lo:2048 + hi] = sw
            return 0

        lax.fori_loop(0, 8, rows, 0)

        def cols(g, _):
            r = pl.multiple_of(g * 16, 16)
            lk = lb[pl.ds(r, 16), :]
            mk = mb[pl.ds(r, 16), :]
            for q in range(4):
                c, s = cos_sin(lk * us[q] + mk * vs[q])
                lanes = slice(q * T, (q + 1) * T)
                right[pl.ds(r, 16), lanes] = c.astype(BF16)
                right[pl.ds(pl.multiple_of(r + 1024, 16), 16), lanes] = s.astype(BF16)
            return 0

        lax.fori_loop(0, 64, cols, 0, unroll=2)
        for n in range(2):
            lanes = slice(n * 256, (n + 1) * 256)
            for z in range(2):
                out = dot(left[:, (1 - z) * 1024:(1 - z) * 1024 + 2048], right[:, lanes], ((1,), (0,)))
                for p in range(2):
                    bo[z, 2 * ch + p, :, lanes] = out[p * T:(p + 1) * T]
        for copy in copies(ch):
            copy.start()
        return 0

    lax.fori_loop(0, 2, chan, 0)
    for ch in range(2):
        for copy in copies(ch):
            copy.wait()


DIAGONAL, SOLVING, PASSING = range(3)


def pack(vis, packed, vin, chunk, in_sem, one_sem, two_sem):
    i, j = lax.axis_index("row"), lax.axis_index("col")
    r, half = i % 4, i // 4
    solving = j == lax.axis_index("chan") % 2
    turn = jnp.where(solving, 0, 4)
    loads = [pltpu.make_async_copy(vis.at[:, k], vin.at[k], in_sem.at[k]) for k in range(8)]
    stores = []
    for k in range(8):
        stores.append(pltpu.make_async_copy(chunk.at[k, :, 0:T], packed.at[k, :, 0:T], one_sem.at[k]))
        stores.append(
            pltpu.make_async_copy(chunk.at[k, :, T:], packed.at[(k + turn) % 8, :, T:], two_sem.at[k])
        )
    for load in loads:
        load.start()
    left = lax.broadcasted_iota(jnp.int32, (32, T), 1) < 64

    def run(place):
        for k in range(8):
            loads[k].wait()

            def block(z, n):
                lane = pl.multiple_of(((r + n) % 4) * T, T)
                return vin[k, z, :, pl.ds(lane, T)]

            for z in range(2):
                if place == DIAGONAL:
                    chunk[k, z, 0:T, :] = block(z, 1)
                    third = block(z, 2)
                    turned = third.T[64:T]
                    chunk[k, z, T:T + 64, :] = jnp.where(r < 2, third[0:64], -turned if z else turned)
                    own = block(z, 0)
                    chunk[k, z, T + 64:2 * T, :] = own[0:64]
                    chunk[k, z, 2 * T:, :] = jnp.where(left, pltpu.roll(own[64:96], 64, 1), own[96:T])
                else:
                    off = jnp.where(half == 1, 1, 0)
                    chunk[k, z, 0:T, :] = block(z, off)
                    second = block(z, off + 1)
                    if place == SOLVING:
                        chunk[k, z, T:2 * T, :] = second
                        chunk[k, z, 2 * T:, :] = block(z, off + 2)[0:32]
                    else:
                        turned = second.T[32:T]
                        chunk[k, z, T:T + 96, :] = -turned if z else turned
                        chunk[k, z, T + 96:, :] = jnp.zeros((64, T), F32)
            stores[2 * k].start()
            stores[2 * k + 1].start()

    @pl.when(half == j)
    def _():
        run(DIAGONAL)

    @pl.when((half != j) & solving)
    def _():
        run(SOLVING)

    @pl.when((half != j) & jnp.logical_not(solving))
    def _():
        run(PASSING)

    for store in stores:
        store.wait()


def is_solver():
    return lax.axis_index("col") == lax.axis_index("chan") % 2


class Filler:
    def __init__(self, side, part_of, m_re, m_im, cc, halves, diag):
        self.refs = m_re, m_im, cc, halves, diag
        self.side, self.part_of = side, part_of

    def products(self, row, col, vr, vi):
        m_re, m_im = self.refs[:2]
        rs = pl.ds(pl.multiple_of(row * T, T), T)
        cs = pl.ds(pl.multiple_of(col * T, T), T)
        mr = m_re[rs, cs]
        mi = m_im[rs, cs]
        return vr * mr + vi * mi, vr * mi - vi * mr

    def put(self, row, col, parts):
        cc = self.refs[2]
        cs = pl.ds(pl.multiple_of(col * T, T), T)
        for n, part in enumerate(parts):
            cc[pl.ds(pl.multiple_of(n * 1024 + row * T, T), T), cs] = part.astype(BF16)

    def fill(self, row, col, vr, vi):
        self.put(row, col, self.products(row, col, vr, vi))
        self.put(col, row, self.products(col, row, vr.T, -vi.T))

    def own_block(self, a, z):
        low = lax.broadcasted_iota(jnp.int32, (64, T), 1) < 64
        top = self.part_of(True, a, z, T + 64, 2 * T)
        turned = jnp.concatenate([top, top], 0).T[64:T]
        last = self.part_of(True, a, z, 2 * T, ROWS)
        right = jnp.concatenate([pltpu.roll(last, 64, 1), last], 0)
        return jnp.concatenate([top, jnp.where(low, -turned if z else turned, right)], 0)

    def run(self):
        part_of, fill = self.part_of, self.fill
        halves, diag = self.refs[3:]
        jj = (lax.axis_index("col") + self.side) % 2
        off = jnp.where(jj == 0, 1, 0)
        eye = on_diagonal()

        def sources(r, _):
            a = 4 * jj + r
            parts = self.products(a, a, self.own_block(a, 0), self.own_block(a, 1))
            for n, part in enumerate(parts):
                diag[pl.ds(8 * n + a, 1), :] = jnp.sum(jnp.where(eye, part, 0.0), axis=0, keepdims=True)
            self.put(a, a, [jnp.where(eye, 0.0, part) for part in parts])
            fill(a, 4 * jj + (r + 1) % 4, part_of(True, a, 0, 0, T), part_of(True, a, 1, 0, T))
            for z in range(2):
                rs = pl.ds(pl.multiple_of((r // 2) * 64, 64), 64)
                halves[z, r % 2, rs, :] = part_of(True, a, z, T, T + 64)
            b = 4 * (1 - jj) + r
            fill(b, 4 * jj + (r + off) % 4, part_of(False, b, 0, 0, T), part_of(False, b, 1, 0, T))
            if self.side == 0:
                fill(b, 4 * jj + (r + off + 1) % 4, part_of(False, b, 0, T, 2 * T), part_of(False, b, 1, T, 2 * T))
            else:
                for z in range(2):
                    halves[z, 2 + (r + off + 1) % 4, 32:T, :] = part_of(False, b, z, T, T + 96)
            return 0

        lax.fori_loop(0, 4, sources, 0)

        def across(p, _):
            fill(4 * jj + p, 4 * jj + p + 2, halves[0, p], halves[1, p])
            return 0

        lax.fori_loop(0, 2, across, 0)


def on_diagonal():
    return lax.broadcasted_iota(jnp.int32, (T, T), 0) == lax.broadcasted_iota(jnp.int32, (T, T), 1)


def of_near(near):
    return lambda diagonal, a, z, lo, hi: near[a, z, lo:hi, :]


def of_far(far1, far2):
    def part_of(diagonal, a, z, lo, hi):
        if hi <= T:
            return far1[a, z, lo:hi, :]
        start = lo - T + (0 if diagonal else ROWS - T)
        return far2[a % 4, z, start:start + hi - lo, :]

    return part_of


def prepare(near, m_re, m_im, cc, diag, halves):
    @pl.when(is_solver())
    def _():
        eye = on_diagonal()

        def powers(a, _):
            rs = pl.ds(pl.multiple_of(a * T, T), T)
            out = pl.ds(pl.multiple_of(2048 + a * T, T), T)
            for t in range(8):
                lanes = slice(t * T, (t + 1) * T)
                mr = m_re[rs, lanes]
                mi = m_im[rs, lanes]
                cc[out, lanes] = (mr * mr + mi * mi).astype(BF16)
            lanes = pl.ds(pl.multiple_of(a * T, T), T)
            mr = m_re[rs, lanes]
            mi = m_im[rs, lanes]
            den = mr * mr + mi * mi
            diag[pl.ds(16 + a, 1), :] = jnp.sum(jnp.where(eye, den, 0.0), axis=0, keepdims=True)
            cc[out, lanes] = jnp.where(eye, 0.0, den).astype(BF16)
            return 0

        lax.fori_loop(0, 8, powers, 0)
        Filler(0, of_near(near), m_re, m_im, cc, halves, diag).run()


def gain_solve(flags, part, part_diag, near, far1, far2, m_re, m_im, out, cc, halves, diag, sem):
    @pl.when(is_solver())
    def _():
        copy = pltpu.make_async_copy(part, cc, sem)
        copy.start()
        diag[...] = part_diag[...]
        copy.wait()
        solve(flags, near, far1, far2, m_re, m_im, out, cc, halves, diag)

    @pl.when(jnp.logical_not(is_solver()))
    def _():
        out[...] = jnp.zeros_like(out)


def solve(flags, near, far1, far2, m_re, m_im, out, cc, halves, diag):
    cp, j = lax.axis_index("row"), lax.axis_index("col")
    filler = Filler(1, of_far(far1, far2), m_re, m_im, cc, halves, diag)
    filler.run()
    near_off = jnp.where(j == 0, 1, 0)

    def thirds(r, _):
        a = 4 * (1 - j) + r
        for z in range(2):
            halves[z, 2 + r, 0:32, :] = near[a, z, 2 * T:ROWS, :]
        filler.fill(a, 4 * j + (r + near_off + 2) % 4, halves[0, 2 + r], halves[1, 2 + r])
        return 0

    lax.fori_loop(0, 4, thirds, 0)
    w = flags[pl.ds(cp // 2, 1), :].astype(F32)

    def row_of(n):
        return jnp.concatenate([diag[8 * n + t:8 * n + t + 1, :] for t in range(8)], 1)

    d_re, d_im, d_den = row_of(0), row_of(1), row_of(2)
    sub = lax.broadcasted_iota(jnp.int32, (16, 1024), 0)

    def split(x):
        return x, x - x.astype(BF16).astype(F32)

    def stack(*rows):
        out = jnp.zeros((16, 1024), F32)
        for n, x in rows:
            out = jnp.where(sub == n, x, out)
        return out

    def one(step, carry):
        g_re, g_im = carry
        hr, hr_lo = split(w * g_re)
        hi, hi_lo = split(w * g_im)
        hd, hd_lo = split(w * (g_re * g_re + g_im * g_im))
        left = jnp.concatenate(
            [
                stack((0, hr), (1, hi), (3, hr_lo), (4, hi_lo)),
                stack((0, -hi), (1, hr), (3, -hi_lo), (4, hr_lo)),
                stack((2, hd), (5, hd_lo)),
            ],
            1,
        ).astype(BF16)
        sums = dot(left, cc[...], ((1,), (0,)))
        num_re = sums[0:1] + sums[3:4] + (hr * d_re - hi * d_im)
        num_im = sums[1:2] + sums[4:5] + (hr * d_im + hi * d_re)
        den = sums[2:3] + sums[5:6] + hd * d_den
        scale = w / (den + 1.0 - w)
        n_re = num_re * scale
        n_im = num_im * scale
        odd = (step % 2) == 1
        return (
            jnp.where(odd, 0.5 * (n_re + g_re), n_re),
            jnp.where(odd, 0.5 * (n_im + g_im), n_im),
        )

    g_re, g_im = lax.fori_loop(0, ITERS, one, (w, jnp.zeros((1, 1024), F32)))
    for n in range(out.shape[0]):
        out[n, 0:1, :] = g_re
        out[n, 1:2, :] = g_im


def residual(vis, re_early, im_early, re_late, im_late, gall, res, gains, o, out_sem):
    i, j = lax.axis_index("row"), lax.axis_index("col")
    active = lax.axis_index("chan") % 2
    stores = [pltpu.make_async_copy(o.at[cp], res.at[:, cp], out_sem.at[cp]) for cp in range(8)]
    for n in range(8):
        for z in range(2):
            gains[z, n // 2, n % 2:n % 2 + 1, :] = gall[2 * n + active, z:z + 1, :]
    for cp in range(8):
        m_re, m_im = (re_early, im_early) if cp < 4 else (re_late, im_late)
        src = 2 * cp + active

        def lanes_of(z, t):
            return gall[src, z:z + 1, pl.ds(pl.multiple_of(t * T, T), T)]

        gpr = jnp.broadcast_to(lanes_of(0, i), (T, T)).T
        gpi = jnp.broadcast_to(lanes_of(1, i), (T, T)).T
        for q in range(4):
            lanes = slice(q * T, (q + 1) * T)
            gqr = lanes_of(0, 4 * j + q)
            gqi = lanes_of(1, 4 * j + q)
            mr = m_re[cp % 4, :, lanes]
            mi = m_im[cp % 4, :, lanes]
            ar = mr * gqr + mi * gqi
            ai = mi * gqr - mr * gqi
            o[cp, 0, :, lanes] = vis[0, cp, :, lanes] - (gpr * ar - gpi * ai)
            o[cp, 1, :, lanes] = vis[1, cp, :, lanes] - (gpr * ai + gpi * ar)
        stores[cp].start()
    for store in stores:
        store.wait()


SMEM = pl.BlockSpec(memory_space=pltpu.SMEM)
VMEM = pl.BlockSpec(memory_space=pltpu.VMEM)
ANY = pl.BlockSpec(memory_space=pl.ANY)


def vmem(mib):
    return pltpu.CompilerParams(vmem_limit_bytes=mib << 20)


def shape(*dims):
    return jax.ShapeDtypeStruct(dims, F32)


def body(rows, cols, chans, visibilities, stations, pixels, flux, freqs, flags):
    vis = visibilities.reshape(2, 8, T, 512)
    st = stations.reshape(2, 8, T)
    pix = pixels.reshape(8, T)
    fx = flux.reshape(8, 8, T)

    with jax.named_scope("pack"):
        packed = pl.pallas_call(
            pack,
            out_shape=shape(8, 2, ROWS, T),
            in_specs=[ANY],
            out_specs=ANY,
            scratch_shapes=[
                pltpu.VMEM((8, 2, T, 512), F32),
                pltpu.VMEM((8, 2, ROWS, T), F32),
                pltpu.SemaphoreType.DMA((8,)),
                pltpu.SemaphoreType.DMA((8,)),
                pltpu.SemaphoreType.DMA((8,)),
            ],
            compiler_params=vmem(60),
            cost_estimate=pl.CostEstimate(flops=1 << 20, bytes_accessed=7 << 20, transcendentals=0),
        )(vis)
    with jax.named_scope("to_the_rows"):
        near = lax.all_to_all(packed, "row", 0, 0, tiled=True)

    with jax.named_scope("own_model"):
        m_re, m_im = pl.pallas_call(
            own_model,
            out_shape=(shape(1024, 1024),) * 2,
            in_specs=[SMEM, VMEM, VMEM, VMEM],
            out_specs=(ANY,) * 2,
            scratch_shapes=[
                pltpu.VMEM((1024, T), F32),
                pltpu.VMEM((1024, T), F32),
                pltpu.VMEM((1024, 2048), BF16),
                pltpu.VMEM((1024, 3072), BF16),
                pltpu.VMEM((2, 1024, 1024), F32),
                pltpu.SemaphoreType.DMA((2, 4)),
            ],
            compiler_params=vmem(60),
            cost_estimate=pl.CostEstimate(flops=8 << 30, bytes_accessed=8 << 20, transcendentals=8 << 20),
        )(freqs, st, pix, fx)
    def block(first):
        return pl.pallas_call(
            functools.partial(block_model, first),
            out_shape=(shape(4, T, 512),) * 2,
            in_specs=[SMEM, VMEM, VMEM, VMEM],
            out_specs=(ANY,) * 2,
            scratch_shapes=[
                pltpu.VMEM((T, T), F32),
                pltpu.VMEM((T, T), F32),
                pltpu.VMEM((1024, T), F32),
                pltpu.VMEM((1024, T), F32),
                pltpu.VMEM((256, 3072), BF16),
                pltpu.VMEM((2048, 512), BF16),
                pltpu.VMEM((2, 4, T, 512), F32),
                pltpu.SemaphoreType.DMA((2, 2)),
            ],
            compiler_params=vmem(14),
            cost_estimate=pl.CostEstimate(flops=4 << 30, bytes_accessed=2 << 20, transcendentals=4 << 20),
        )(freqs, st, pix, fx)

    with jax.named_scope("to_the_active_column"):
        near, m_re, m_im, *early = lax.optimization_barrier((near, m_re, m_im, *block(0)))
        mine = 4 * lax.axis_index("col")
        pieces = [
            near[:, :, 0:T],
            jnp.concatenate(
                [
                    lax.dynamic_slice_in_dim(near, mine, 4)[:, :, T:ROWS],
                    lax.dynamic_slice_in_dim(near, 4 - mine, 4)[:, :, T:T + 96],
                ],
                2,
            ),
        ]
        far = []
        for piece, turn in zip(pieces, (0, rows // 2)):
            pairs = []
            for z in range(chans):
                to = z % 2
                for r in range(rows):
                    src = (r * cols + 1 - to) * chans + z
                    dst = ((r + turn) % rows * cols + to) * chans + z
                    pairs.append((src, dst))
            far.append(lax.ppermute(piece, ("row", "col", "chan"), pairs))

    with jax.named_scope("block_model"):
        late = block(2)
    with jax.named_scope("prepare"):
        part, part_diag = pl.pallas_call(
            prepare,
            out_shape=(jax.ShapeDtypeStruct((3072, 1024), BF16), shape(24, T)),
            in_specs=[VMEM] * 3,
            out_specs=(VMEM, VMEM),
            scratch_shapes=[pltpu.VMEM((2, 2, T, T), F32)],
            compiler_params=vmem(18),
            cost_estimate=pl.CostEstimate(flops=16 << 20, bytes_accessed=16 << 20, transcendentals=0),
        )(near, m_re, m_im)
    far[0], far[1], part, *late = lax.optimization_barrier((far[0], far[1], part, *late))

    with jax.named_scope("gain_solve"):
        g = pl.pallas_call(
            gain_solve,
            out_shape=shape(rows * cols, 2, 1024),
            in_specs=[VMEM] * 8,
            out_specs=VMEM,
            scratch_shapes=[
                pltpu.VMEM((3072, 1024), BF16),
                pltpu.VMEM((2, 6, T, T), F32),
                pltpu.VMEM((24, T), F32),
                pltpu.SemaphoreType.DMA,
            ],
            compiler_params=vmem(27),
            cost_estimate=pl.CostEstimate(flops=800 << 20, bytes_accessed=14 << 20, transcendentals=0),
        )(flags, part, part_diag, near, *far, m_re, m_im)

    with jax.named_scope("gather_gains"):
        gall = lax.all_to_all(g, ("row", "col"), 0, 0, tiled=True)

    with jax.named_scope("residual"):
        res, gains = pl.pallas_call(
            residual,
            out_shape=(shape(2, 8, T, 512), shape(2, 4, 2, 1024)),
            in_specs=[VMEM] * 6,
            out_specs=(ANY, VMEM),
            scratch_shapes=[pltpu.VMEM((8, 2, T, 512), F32), pltpu.SemaphoreType.DMA((8,))],
            compiler_params=vmem(14),
            cost_estimate=pl.CostEstimate(flops=32 << 20, bytes_accessed=12 << 20, transcendentals=0),
        )(vis, *early, *late, gall)
    return gains, res.reshape(2, 4, 2, T, 512)


def solution(mesh):
    in_specs = (
        P(None, "chan", None, "row", "col"),
        P(None, "chan"),
        P("chan"),
        P("chan", None, None),
        P("chan"),
        P("chan", None),
    )
    out_specs = (P(None, "chan", None, None), P(None, "chan", None, "row", "col"))
    run = functools.partial(body, mesh.shape["row"], mesh.shape["col"], mesh.shape["chan"])
    return jax.shard_map(run, mesh=mesh, in_specs=in_specs, out_specs=out_specs, check_vma=False)
```

```python
import functools

import jax
import jax.numpy as jnp
from jax import lax
from jax.experimental import pallas as pl
from jax.experimental.pallas import tpu as pltpu
from jax.sharding import PartitionSpec as P

ITERS = 8
SIDE = 1024
T = 128

SIN = (4.442867982256445, -7.307445413087933, 3.5948021037170865, -0.7844036262695797)
COS = (1.4142040804669562, -6.977642056688731, 5.715238393830307, -1.728348659759922)
MAGIC = 12582912.0
F32 = jnp.float32
BF16 = jnp.bfloat16
ROWS = 272
SPLIT = 136
THIRD = 16


def poly(y, coeffs):
    out = coeffs[-1]
    for c in reversed(coeffs[:-1]):
        out = out * y + c
    return out


def cos_sin(turns):
    r = turns - ((turns + MAGIC) - MAGIC)
    y = r * r
    s = r * poly(y, SIN)
    c = poly(y, COS)
    return 1.0 - s * s, s * c


def lm_rows(pix):
    across = (pix & (SIDE - 1)).astype(F32)
    down = (pix >> 10).astype(F32)
    lv = (across + 0.5) / SIDE * 0.5 - 0.25
    mv = (down + 0.5) / SIDE * 0.5 - 0.25
    return lv, mv


def spread(rows, out_ref):
    for t in range(8):
        out_ref[t * T:(t + 1) * T, :] = jnp.broadcast_to(rows[t:t + 1, :], (T, T)).T


def dot(a, b, dims):
    return lax.dot_general(a, b, (dims, ((), ())), preferred_element_type=F32)


def own_model(freqs, st, pix, flux, own_re, own_im, ub, vb, left, right, oo, sem):
    i = lax.axis_index("row")

    @pl.when(lax.axis_index("col") == lax.axis_index("chan") % 2)
    def _():
        f = freqs[i // 2]
        lv, mv = lm_rows(pix[...])
        spread(st[0] * f, ub)
        spread(st[1] * f, vb)
        fx = flux[i]

        def waves(g, _):
            r = pl.multiple_of(g * 16, 16)
            u = ub[pl.ds(r, 16), :]
            v = vb[pl.ds(r, 16), :]
            for k in range(8):
                c, s = cos_sin(u * lv[k:k + 1, :] + v * mv[k:k + 1, :])
                w = fx[k:k + 1, :]
                lo, hi = k * T, (k + 1) * T
                left[pl.ds(r, 16), lo:hi] = (c * w).astype(BF16)
                left[pl.ds(r, 16), 1024 + lo:1024 + hi] = (s * w).astype(BF16)
                cb = c.astype(BF16)
                right[pl.ds(r, 16), lo:hi] = cb
                right[pl.ds(r, 16), 1024 + lo:1024 + hi] = s.astype(BF16)
                right[pl.ds(r, 16), 2048 + lo:2048 + hi] = -cb
            return 0

        lax.fori_loop(0, 64, waves, 0)

        def copies(m):
            rs = pl.ds(pl.multiple_of(m * 256, 256), 256)
            return [pltpu.make_async_copy(oo.at[z, rs], (own_re, own_im)[z].at[rs], sem.at[z, m]) for z in range(2)]

        def rows(m, _):
            rs = pl.ds(pl.multiple_of(m * 256, 256), 256)
            for n in range(2):
                cs = slice(n * 512, (n + 1) * 512)
                for z in range(2):
                    oo[z, rs, cs] = dot(left[rs, :], right[cs, z * 1024:z * 1024 + 2048], ((1,), (1,)))
            for copy in copies(m):
                copy.start()
            return 0

        lax.fori_loop(0, 4, rows, 0)
        for m in range(4):
            for copy in copies(m):
                copy.wait()


def block_model(first, freqs, st, pix, flux, blk_re, blk_im, rub, rvb, lb, mb, left, right, bo, sem):
    i, j = lax.axis_index("row"), lax.axis_index("col")
    lv, mv = lm_rows(pix[...])
    spread(lv, lb)
    spread(mv, mb)
    rub[...] = jnp.broadcast_to(st[0, pl.ds(i, 1), :], (T, T)).T
    rvb[...] = jnp.broadcast_to(st[1, pl.ds(i, 1), :], (T, T)).T

    def copies(ch):
        rs = pl.ds(2 * ch, 2)
        return [pltpu.make_async_copy(bo.at[z, rs], (blk_re, blk_im)[z].at[rs], sem.at[z, ch]) for z in range(2)]

    def chan(ch, _):
        f = freqs[first + ch]
        fluxes = [flux[2 * (first + ch) + p] for p in range(2)]
        us = [st[0, pl.ds(4 * j + q, 1), :] * f for q in range(4)]
        vs = [st[1, pl.ds(4 * j + q, 1), :] * f for q in range(4)]

        def rows(g, _):
            r = pl.multiple_of(g * 16, 16)
            u = rub[pl.ds(r, 16), :] * f
            v = rvb[pl.ds(r, 16), :] * f
            for k in range(8):
                c, s = cos_sin(u * lv[k:k + 1, :] + v * mv[k:k + 1, :])
                lo, hi = k * T, (k + 1) * T
                for p in range(2):
                    w = fluxes[p][k:k + 1, :]
                    rs = pl.ds(pl.multiple_of(r + p * T, 16), 16)
                    sw = (s * w).astype(BF16)
                    left[rs, lo:hi] = -sw
                    left[rs, 1024 + lo:1024 + hi] = (c * w).astype(BF16)
                    left[rs, 2048 + lo:2048 + hi] = sw
            return 0

        lax.fori_loop(0, 8, rows, 0)

        def cols(g, _):
            r = pl.multiple_of(g * 16, 16)
            lk = lb[pl.ds(r, 16), :]
            mk = mb[pl.ds(r, 16), :]
            for q in range(4):
                c, s = cos_sin(lk * us[q] + mk * vs[q])
                lanes = slice(q * T, (q + 1) * T)
                right[pl.ds(r, 16), lanes] = c.astype(BF16)
                right[pl.ds(pl.multiple_of(r + 1024, 16), 16), lanes] = s.astype(BF16)
            return 0

        lax.fori_loop(0, 64, cols, 0, unroll=2)
        for n in range(2):
            lanes = slice(n * 256, (n + 1) * 256)
            for z in range(2):
                out = dot(left[:, (1 - z) * 1024:(1 - z) * 1024 + 2048], right[:, lanes], ((1,), (0,)))
                for p in range(2):
                    bo[z, 2 * ch + p, :, lanes] = out[p * T:(p + 1) * T]
        for copy in copies(ch):
            copy.start()
        return 0

    lax.fori_loop(0, 2, chan, 0)
    for ch in range(2):
        for copy in copies(ch):
            copy.wait()


DIAGONAL, SOLVING, PASSING = range(3)


def pack(vis, packed, vin, chunk, in_sem, one_sem, two_sem):
    i, j = lax.axis_index("row"), lax.axis_index("col")
    r, half = i % 4, i // 4
    solving = j == lax.axis_index("chan") % 2
    turn = jnp.where(solving, 0, 4)
    base = jnp.where((half == 1) & (j == 0), 1, 0)
    lanes = [pl.ds(pl.multiple_of((r + base + n) % 4 * T, T), T) for n in range(3)]
    loads = [
        pltpu.make_async_copy(vis.at[:, k, :, lanes[n]], vin.at[k, n], in_sem.at[k, n])
        for k in range(8)
        for n in range(3)
    ]
    stores = []
    for k in range(8):
        stores.append(pltpu.make_async_copy(chunk.at[k, :, 0:SPLIT], packed.at[k, :, 0:SPLIT], one_sem.at[k]))
        stores.append(
            pltpu.make_async_copy(chunk.at[k, :, SPLIT:], packed.at[(k + turn) % 8, :, SPLIT:], two_sem.at[k])
        )
    for load in loads:
        load.start()
    lane = lax.broadcasted_iota(jnp.int32, (32, T), 1)

    def run(place):
        for k in range(8):
            for load in loads[3 * k:3 * k + 3]:
                load.wait()

            def block(z, n):
                return vin[k, n, z]

            for z in range(2):
                if place == DIAGONAL:
                    chunk[k, z, 0:T, :] = block(z, 1)
                    third = block(z, 2)
                    turned = third.T[64:T]
                    chunk[k, z, T:T + 64, :] = jnp.where(r < 2, third[0:64], -turned if z else turned)
                    own = block(z, 0)
                    chunk[k, z, 192:224, :] = own[0:32]
                    chunk[k, z, 224:256, :] = jnp.where(lane < 32, pltpu.roll(own[96:T], 32, 1), own[32:64])
                    chunk[k, z, 256:, :] = jnp.where(lane[0:16] < 64, pltpu.roll(own[80:96], 64, 1), own[64:80])
                else:
                    chunk[k, z, 0:T, :] = block(z, 0)
                    second = block(z, 1)
                    if place == SOLVING:
                        chunk[k, z, T:2 * T, :] = second
                        chunk[k, z, 2 * T:, :] = block(z, 2)[0:THIRD]
                    else:
                        turned = second.T[THIRD:T]
                        chunk[k, z, T:2 * T - THIRD, :] = -turned if z else turned
                        chunk[k, z, 2 * T - THIRD:, :] = jnp.zeros((2 * THIRD, T), F32)
            stores[2 * k].start()
            stores[2 * k + 1].start()

    @pl.when(half == j)
    def _():
        run(DIAGONAL)

    @pl.when((half != j) & solving)
    def _():
        run(SOLVING)

    @pl.when((half != j) & jnp.logical_not(solving))
    def _():
        run(PASSING)

    for store in stores:
        store.wait()


def is_solver():
    return lax.axis_index("col") == lax.axis_index("chan") % 2


class Filler:
    def __init__(self, side, part_of, m_re, m_im, cc, halves, diag):
        self.refs = m_re, m_im, cc, halves, diag
        self.side, self.part_of = side, part_of

    def products(self, row, col, vr, vi):
        m_re, m_im = self.refs[:2]
        rs = pl.ds(pl.multiple_of(row * T, T), T)
        cs = pl.ds(pl.multiple_of(col * T, T), T)
        mr = m_re[rs, cs]
        mi = m_im[rs, cs]
        return vr * mr + vi * mi, vr * mi - vi * mr

    def put(self, row, col, parts):
        cc = self.refs[2]
        cs = pl.ds(pl.multiple_of(col * T, T), T)
        for n, part in enumerate(parts):
            cc[pl.ds(pl.multiple_of(n * 1024 + row * T, T), T), cs] = part.astype(BF16)

    def fill(self, row, col, vr, vi):
        self.put(row, col, self.products(row, col, vr, vi))
        self.put(col, row, self.products(col, row, vr.T, -vi.T))

    def own_block(self, a, z):
        row = lax.broadcasted_iota(jnp.int32, (T, T), 0)
        lane = lax.broadcasted_iota(jnp.int32, (T, T), 1)
        one = self.part_of(True, a, z, 192, 224)
        two = self.part_of(True, a, z, 224, 256)
        three = self.part_of(True, a, z, 256, ROWS)
        upper = jnp.concatenate([one, two, three, pltpu.roll(three, 64, 1), pltpu.roll(two, 96, 1)], 0)
        turned = upper.T
        return jnp.where((lane >> 5) >= (row >> 5), upper, -turned if z else turned)

    def run(self):
        part_of, fill = self.part_of, self.fill
        halves, diag = self.refs[3:]
        jj = (lax.axis_index("col") + self.side) % 2
        off = jnp.where(jj == 0, 1, 0)
        eye = on_diagonal()

        def sources(r, _):
            a = 4 * jj + r
            parts = self.products(a, a, self.own_block(a, 0), self.own_block(a, 1))
            for n, part in enumerate(parts):
                diag[pl.ds(8 * n + a, 1), :] = jnp.sum(jnp.where(eye, part, 0.0), axis=0, keepdims=True)
            self.put(a, a, [jnp.where(eye, 0.0, part) for part in parts])
            fill(a, 4 * jj + (r + 1) % 4, part_of(True, a, 0, 0, T), part_of(True, a, 1, 0, T))
            for z in range(2):
                rs = pl.ds(pl.multiple_of((r // 2) * 64, 64), 64)
                halves[z, r % 2, rs, :] = part_of(True, a, z, T, T + 64)
            b = 4 * (1 - jj) + r
            fill(b, 4 * jj + (r + off) % 4, part_of(False, b, 0, 0, T), part_of(False, b, 1, 0, T))
            if self.side == 0:
                fill(b, 4 * jj + (r + off + 1) % 4, part_of(False, b, 0, T, 2 * T), part_of(False, b, 1, T, 2 * T))
            else:
                for z in range(2):
                    halves[z, 2 + (r + off + 1) % 4, THIRD:T, :] = part_of(False, b, z, T, 2 * T - THIRD)
            return 0

        lax.fori_loop(0, 4, sources, 0)

        def across(p, _):
            fill(4 * jj + p, 4 * jj + p + 2, halves[0, p], halves[1, p])
            return 0

        lax.fori_loop(0, 2, across, 0)


def on_diagonal():
    return lax.broadcasted_iota(jnp.int32, (T, T), 0) == lax.broadcasted_iota(jnp.int32, (T, T), 1)


def of_near(near):
    return lambda diagonal, a, z, lo, hi: near[a, z, lo:hi, :]


def of_far(far1, far2):
    def part_of(diagonal, a, z, lo, hi):
        parts = []
        if lo < SPLIT:
            parts.append(far1[a, z, lo:min(hi, SPLIT), :])
        if hi > SPLIT:
            start = max(lo, SPLIT)
            at = start - SPLIT + (0 if diagonal else ROWS - SPLIT)
            parts.append(far2[a % 4, z, at:at + hi - start, :])
        return parts[0] if len(parts) == 1 else jnp.concatenate(parts, 0)

    return part_of


def prepare(near, m_re, m_im, cc, diag, halves):
    @pl.when(is_solver())
    def _():
        eye = on_diagonal()

        def powers(a, _):
            rs = pl.ds(pl.multiple_of(a * T, T), T)
            out = pl.ds(pl.multiple_of(2048 + a * T, T), T)
            for t in range(8):
                lanes = slice(t * T, (t + 1) * T)
                mr = m_re[rs, lanes]
                mi = m_im[rs, lanes]
                cc[out, lanes] = (mr * mr + mi * mi).astype(BF16)
            lanes = pl.ds(pl.multiple_of(a * T, T), T)
            mr = m_re[rs, lanes]
            mi = m_im[rs, lanes]
            den = mr * mr + mi * mi
            diag[pl.ds(16 + a, 1), :] = jnp.sum(jnp.where(eye, den, 0.0), axis=0, keepdims=True)
            cc[out, lanes] = jnp.where(eye, 0.0, den).astype(BF16)
            return 0

        lax.fori_loop(0, 8, powers, 0)
        Filler(0, of_near(near), m_re, m_im, cc, halves, diag).run()


def gain_solve(flags, part, part_diag, near, far1, far2, m_re, m_im, out, cc, halves, diag, sem):
    @pl.when(is_solver())
    def _():
        copy = pltpu.make_async_copy(part.at[0:2048], cc, sem)
        copy.start()
        diag[...] = part_diag[...]
        copy.wait()
        solve(flags, part, near, far1, far2, m_re, m_im, out, cc, halves, diag)

    @pl.when(jnp.logical_not(is_solver()))
    def _():
        out[...] = jnp.zeros_like(out)


def solve(flags, part, near, far1, far2, m_re, m_im, out, cc, halves, diag):
    cp, j = lax.axis_index("row"), lax.axis_index("col")
    filler = Filler(1, of_far(far1, far2), m_re, m_im, cc, halves, diag)
    filler.run()
    near_off = jnp.where(j == 0, 1, 0)

    def thirds(r, _):
        a = 4 * (1 - j) + r
        for z in range(2):
            halves[z, 2 + r, 0:THIRD, :] = near[a, z, 2 * T:ROWS, :]
        filler.fill(a, 4 * j + (r + near_off + 2) % 4, halves[0, 2 + r], halves[1, 2 + r])
        return 0

    lax.fori_loop(0, 4, thirds, 0)
    w = flags[pl.ds(cp // 2, 1), :].astype(F32)

    def row_of(n):
        return jnp.concatenate([diag[8 * n + t:8 * n + t + 1, :] for t in range(8)], 1)

    d_re, d_im, d_den = row_of(0), row_of(1), row_of(2)
    sub = lax.broadcasted_iota(jnp.int32, (16, 1024), 0)

    def split(x):
        return x, x - x.astype(BF16).astype(F32)

    def stack(*rows):
        out = jnp.zeros((16, 1024), F32)
        for n, x in rows:
            out = jnp.where(sub == n, x, out)
        return out

    def one(step, carry):
        g_re, g_im = carry
        hr, hr_lo = split(w * g_re)
        hi, hi_lo = split(w * g_im)
        hd, hd_lo = split(w * (g_re * g_re + g_im * g_im))
        left = jnp.concatenate(
            [
                stack((0, hr), (1, hi), (3, hr_lo), (4, hi_lo)),
                stack((0, -hi), (1, hr), (3, -hi_lo), (4, hr_lo)),
            ],
            1,
        ).astype(BF16)
        powers = stack((2, hd), (5, hd_lo)).astype(BF16)
        sums = dot(left, cc[...], ((1,), (0,))) + dot(powers, part[2048:3072, :], ((1,), (0,)))
        num_re = sums[0:1] + sums[3:4] + (hr * d_re - hi * d_im)
        num_im = sums[1:2] + sums[4:5] + (hr * d_im + hi * d_re)
        den = sums[2:3] + sums[5:6] + hd * d_den
        scale = w / (den + 1.0 - w)
        n_re = num_re * scale
        n_im = num_im * scale
        odd = (step % 2) == 1
        return (
            jnp.where(odd, 0.5 * (n_re + g_re), n_re),
            jnp.where(odd, 0.5 * (n_im + g_im), n_im),
        )

    g_re, g_im = lax.fori_loop(0, ITERS, one, (w, jnp.zeros((1, 1024), F32)))
    for n in range(out.shape[0]):
        out[n, 0:1, :] = g_re
        out[n, 1:2, :] = g_im


def residual(vis, re_early, im_early, re_late, im_late, gall, res, gains, o, out_sem):
    i, j = lax.axis_index("row"), lax.axis_index("col")
    active = lax.axis_index("chan") % 2
    stores = [pltpu.make_async_copy(o.at[cp], res.at[:, cp], out_sem.at[cp]) for cp in range(8)]
    for n in range(8):
        for z in range(2):
            gains[z, n // 2, n % 2:n % 2 + 1, :] = gall[2 * n + active, z:z + 1, :]
    for cp in range(8):
        m_re, m_im = (re_early, im_early) if cp < 4 else (re_late, im_late)
        src = 2 * cp + active

        def lanes_of(z, t):
            return gall[src, z:z + 1, pl.ds(pl.multiple_of(t * T, T), T)]

        gpr = jnp.broadcast_to(lanes_of(0, i), (T, T)).T
        gpi = jnp.broadcast_to(lanes_of(1, i), (T, T)).T
        for q in range(4):
            lanes = slice(q * T, (q + 1) * T)
            gqr = lanes_of(0, 4 * j + q)
            gqi = lanes_of(1, 4 * j + q)
            mr = m_re[cp % 4, :, lanes]
            mi = m_im[cp % 4, :, lanes]
            ar = mr * gqr + mi * gqi
            ai = mi * gqr - mr * gqi
            o[cp, 0, :, lanes] = vis[0, cp, :, lanes] - (gpr * ar - gpi * ai)
            o[cp, 1, :, lanes] = vis[1, cp, :, lanes] - (gpr * ai + gpi * ar)
        stores[cp].start()
    for store in stores:
        store.wait()


SMEM = pl.BlockSpec(memory_space=pltpu.SMEM)
VMEM = pl.BlockSpec(memory_space=pltpu.VMEM)
ANY = pl.BlockSpec(memory_space=pl.ANY)


def vmem(mib):
    return pltpu.CompilerParams(vmem_limit_bytes=mib << 20)


def shape(*dims):
    return jax.ShapeDtypeStruct(dims, F32)


def body(rows, cols, chans, visibilities, stations, pixels, flux, freqs, flags):
    vis = visibilities.reshape(2, 8, T, 512)
    st = stations.reshape(2, 8, T)
    pix = pixels.reshape(8, T)
    fx = flux.reshape(8, 8, T)

    with jax.named_scope("pack"):
        packed = pl.pallas_call(
            pack,
            out_shape=shape(8, 2, ROWS, T),
            in_specs=[ANY],
            out_specs=ANY,
            scratch_shapes=[
                pltpu.VMEM((8, 3, 2, T, T), F32),
                pltpu.VMEM((8, 2, ROWS, T), F32),
                pltpu.SemaphoreType.DMA((8, 3)),
                pltpu.SemaphoreType.DMA((8,)),
                pltpu.SemaphoreType.DMA((8,)),
            ],
            compiler_params=vmem(60),
            cost_estimate=pl.CostEstimate(flops=1 << 20, bytes_accessed=7 << 20, transcendentals=0),
        )(vis)
    with jax.named_scope("to_the_rows"):
        near = lax.all_to_all(packed, "row", 0, 0, tiled=True)

    with jax.named_scope("own_model"):
        m_re, m_im = pl.pallas_call(
            own_model,
            out_shape=(shape(1024, 1024),) * 2,
            in_specs=[SMEM, VMEM, VMEM, VMEM],
            out_specs=(ANY,) * 2,
            scratch_shapes=[
                pltpu.VMEM((1024, T), F32),
                pltpu.VMEM((1024, T), F32),
                pltpu.VMEM((1024, 2048), BF16),
                pltpu.VMEM((1024, 3072), BF16),
                pltpu.VMEM((2, 1024, 1024), F32),
                pltpu.SemaphoreType.DMA((2, 4)),
            ],
            compiler_params=vmem(60),
            cost_estimate=pl.CostEstimate(flops=8 << 30, bytes_accessed=8 << 20, transcendentals=8 << 20),
        )(freqs, st, pix, fx)
    def block(first):
        return pl.pallas_call(
            functools.partial(block_model, first),
            out_shape=(shape(4, T, 512),) * 2,
            in_specs=[SMEM, VMEM, VMEM, VMEM],
            out_specs=(ANY,) * 2,
            scratch_shapes=[
                pltpu.VMEM((T, T), F32),
                pltpu.VMEM((T, T), F32),
                pltpu.VMEM((1024, T), F32),
                pltpu.VMEM((1024, T), F32),
                pltpu.VMEM((256, 3072), BF16),
                pltpu.VMEM((2048, 512), BF16),
                pltpu.VMEM((2, 4, T, 512), F32),
                pltpu.SemaphoreType.DMA((2, 2)),
            ],
            compiler_params=vmem(14),
            cost_estimate=pl.CostEstimate(flops=4 << 30, bytes_accessed=2 << 20, transcendentals=4 << 20),
        )(freqs, st, pix, fx)

    with jax.named_scope("to_the_active_column"):
        near, m_re, m_im, *early = lax.optimization_barrier((near, m_re, m_im, *block(0)))
        mine = 4 * lax.axis_index("col")
        pieces = [
            near[:, :, 0:SPLIT],
            jnp.concatenate(
                [
                    lax.dynamic_slice_in_dim(near, mine, 4)[:, :, SPLIT:ROWS],
                    lax.dynamic_slice_in_dim(near, 4 - mine, 4)[:, :, SPLIT:2 * T - THIRD],
                ],
                2,
            ),
        ]
        far = []
        for piece, turn in zip(pieces, (0, rows // 2)):
            pairs = []
            for z in range(chans):
                to = z % 2
                for r in range(rows):
                    src = (r * cols + 1 - to) * chans + z
                    dst = ((r + turn) % rows * cols + to) * chans + z
                    pairs.append((src, dst))
            far.append(lax.ppermute(piece, ("row", "col", "chan"), pairs))

    with jax.named_scope("block_model"):
        late = block(2)
    with jax.named_scope("prepare"):
        part, part_diag = pl.pallas_call(
            prepare,
            out_shape=(jax.ShapeDtypeStruct((3072, 1024), BF16), shape(24, T)),
            in_specs=[VMEM] * 3,
            out_specs=(VMEM, VMEM),
            scratch_shapes=[pltpu.VMEM((2, 2, T, T), F32)],
            compiler_params=vmem(18),
            cost_estimate=pl.CostEstimate(flops=16 << 20, bytes_accessed=16 << 20, transcendentals=0),
        )(near, m_re, m_im)
    far[0], far[1], part, *late = lax.optimization_barrier((far[0], far[1], part, *late))

    with jax.named_scope("gain_solve"):
        g = pl.pallas_call(
            gain_solve,
            out_shape=shape(rows * cols, 2, 1024),
            in_specs=[VMEM] * 8,
            out_specs=VMEM,
            scratch_shapes=[
                pltpu.VMEM((2048, 1024), BF16),
                pltpu.VMEM((2, 6, T, T), F32),
                pltpu.VMEM((24, T), F32),
                pltpu.SemaphoreType.DMA,
            ],
            compiler_params=vmem(27),
            cost_estimate=pl.CostEstimate(flops=800 << 20, bytes_accessed=14 << 20, transcendentals=0),
        )(flags, part, part_diag, near, *far, m_re, m_im)

    with jax.named_scope("gather_gains"):
        gall = lax.all_to_all(g, ("row", "col"), 0, 0, tiled=True)

    with jax.named_scope("residual"):
        res, gains = pl.pallas_call(
            residual,
            out_shape=(shape(2, 8, T, 512), shape(2, 4, 2, 1024)),
            in_specs=[VMEM] * 6,
            out_specs=(ANY, VMEM),
            scratch_shapes=[pltpu.VMEM((8, 2, T, 512), F32), pltpu.SemaphoreType.DMA((8,))],
            compiler_params=vmem(14),
            cost_estimate=pl.CostEstimate(flops=32 << 20, bytes_accessed=12 << 20, transcendentals=0),
        )(vis, *early, *late, gall)
    return gains, res.reshape(2, 4, 2, T, 512)


def solution(mesh):
    in_specs = (
        P(None, "chan", None, "row", "col"),
        P(None, "chan"),
        P("chan"),
        P("chan", None, None),
        P("chan"),
        P("chan", None),
    )
    out_specs = (P(None, "chan", None, None), P(None, "chan", None, "row", "col"))
    run = functools.partial(body, mesh.shape["row"], mesh.shape["col"], mesh.shape["chan"])
    return jax.shard_map(run, mesh=mesh, in_specs=in_specs, out_specs=out_specs, check_vma=False)
```

```python
import functools

import jax
import jax.numpy as jnp
from jax import lax
from jax.experimental import pallas as pl
from jax.experimental.pallas import tpu as pltpu
from jax.sharding import PartitionSpec as P

ITERS = 8
SIDE = 1024
T = 128

SIN = (4.442867982256445, -7.307445413087933, 3.5948021037170865, -0.7844036262695797)
COS = (1.4142040804669562, -6.977642056688731, 5.715238393830307, -1.728348659759922)
MAGIC = 12582912.0
F32 = jnp.float32
BF16 = jnp.bfloat16
ROWS = 272
SPLIT = 136
THIRD = 16


def poly(y, coeffs):
    out = coeffs[-1]
    for c in reversed(coeffs[:-1]):
        out = out * y + c
    return out


def cos_sin(turns):
    r = turns - ((turns + MAGIC) - MAGIC)
    y = r * r
    s = r * poly(y, SIN)
    c = poly(y, COS)
    return 1.0 - s * s, s * c


def lm_rows(pix):
    across = (pix & (SIDE - 1)).astype(F32)
    down = (pix >> 10).astype(F32)
    lv = (across + 0.5) / SIDE * 0.5 - 0.25
    mv = (down + 0.5) / SIDE * 0.5 - 0.25
    return lv, mv


def spread(rows, out_ref):
    for t in range(8):
        out_ref[t * T:(t + 1) * T, :] = jnp.broadcast_to(rows[t:t + 1, :], (T, T)).T


def dot(a, b, dims):
    return lax.dot_general(a, b, (dims, ((), ())), preferred_element_type=F32)


def own_model(freqs, st, pix, flux, own_re, own_im, ub, vb, left, right, oo, sem):
    i = lax.axis_index("row")

    @pl.when(lax.axis_index("col") == lax.axis_index("chan") % 2)
    def _():
        f = freqs[i // 2]
        lv, mv = lm_rows(pix[...])
        spread(st[0] * f, ub)
        spread(st[1] * f, vb)
        fx = flux[i]

        def waves(g, _):
            r = pl.multiple_of(g * 16, 16)
            u = ub[pl.ds(r, 16), :]
            v = vb[pl.ds(r, 16), :]
            for k in range(8):
                c, s = cos_sin(u * lv[k:k + 1, :] + v * mv[k:k + 1, :])
                w = fx[k:k + 1, :]
                lo, hi = k * T, (k + 1) * T
                left[pl.ds(r, 16), lo:hi] = (c * w).astype(BF16)
                left[pl.ds(r, 16), 1024 + lo:1024 + hi] = (s * w).astype(BF16)
                cb = c.astype(BF16)
                right[pl.ds(r, 16), lo:hi] = cb
                right[pl.ds(r, 16), 1024 + lo:1024 + hi] = s.astype(BF16)
                right[pl.ds(r, 16), 2048 + lo:2048 + hi] = -cb
            return 0

        lax.fori_loop(0, 64, waves, 0)

        def copies(m):
            rs = pl.ds(pl.multiple_of(m * 256, 256), 256)
            return [pltpu.make_async_copy(oo.at[z, rs], (own_re, own_im)[z].at[rs], sem.at[z, m]) for z in range(2)]

        def rows(m, _):
            rs = pl.ds(pl.multiple_of(m * 256, 256), 256)
            for n in range(2):
                cs = slice(n * 512, (n + 1) * 512)
                for z in range(2):
                    oo[z, rs, cs] = dot(left[rs, :], right[cs, z * 1024:z * 1024 + 2048], ((1,), (1,)))
            for copy in copies(m):
                copy.start()
            return 0

        lax.fori_loop(0, 4, rows, 0)
        for m in range(4):
            for copy in copies(m):
                copy.wait()


def block_model(first, freqs, st, pix, flux, blk_re, blk_im, rub, rvb, lb, mb, left, right, bo, sem):
    i, j = lax.axis_index("row"), lax.axis_index("col")
    lv, mv = lm_rows(pix[...])
    spread(lv, lb)
    spread(mv, mb)
    rub[...] = jnp.broadcast_to(st[0, pl.ds(i, 1), :], (T, T)).T
    rvb[...] = jnp.broadcast_to(st[1, pl.ds(i, 1), :], (T, T)).T

    def copies(ch):
        rs = pl.ds(2 * ch, 2)
        return [pltpu.make_async_copy(bo.at[z, rs], (blk_re, blk_im)[z].at[rs], sem.at[z, ch]) for z in range(2)]

    def chan(ch, _):
        f = freqs[first + ch]
        fluxes = [flux[2 * (first + ch) + p] for p in range(2)]
        us = [st[0, pl.ds(4 * j + q, 1), :] * f for q in range(4)]
        vs = [st[1, pl.ds(4 * j + q, 1), :] * f for q in range(4)]

        def rows(g, _):
            r = pl.multiple_of(g * 16, 16)
            u = rub[pl.ds(r, 16), :] * f
            v = rvb[pl.ds(r, 16), :] * f
            for k in range(8):
                c, s = cos_sin(u * lv[k:k + 1, :] + v * mv[k:k + 1, :])
                lo, hi = k * T, (k + 1) * T
                for p in range(2):
                    w = fluxes[p][k:k + 1, :]
                    rs = pl.ds(pl.multiple_of(r + p * T, 16), 16)
                    sw = (s * w).astype(BF16)
                    left[rs, lo:hi] = -sw
                    left[rs, 1024 + lo:1024 + hi] = (c * w).astype(BF16)
                    left[rs, 2048 + lo:2048 + hi] = sw
            return 0

        lax.fori_loop(0, 8, rows, 0)

        def cols(g, _):
            r = pl.multiple_of(g * 16, 16)
            lk = lb[pl.ds(r, 16), :]
            mk = mb[pl.ds(r, 16), :]
            for q in range(4):
                c, s = cos_sin(lk * us[q] + mk * vs[q])
                lanes = slice(q * T, (q + 1) * T)
                right[pl.ds(r, 16), lanes] = c.astype(BF16)
                right[pl.ds(pl.multiple_of(r + 1024, 16), 16), lanes] = s.astype(BF16)
            return 0

        lax.fori_loop(0, 64, cols, 0, unroll=2)
        for n in range(2):
            lanes = slice(n * 256, (n + 1) * 256)
            for z in range(2):
                out = dot(left[:, (1 - z) * 1024:(1 - z) * 1024 + 2048], right[:, lanes], ((1,), (0,)))
                for p in range(2):
                    bo[z, 2 * ch + p, :, lanes] = out[p * T:(p + 1) * T]
        for copy in copies(ch):
            copy.start()
        return 0

    lax.fori_loop(0, 2, chan, 0)
    for ch in range(2):
        for copy in copies(ch):
            copy.wait()


DIAGONAL, SOLVING, PASSING = range(3)


def pack(vis, packed, vin, chunk, in_sem, one_sem, two_sem):
    i, j = lax.axis_index("row"), lax.axis_index("col")
    r, half = i % 4, i // 4
    solving = j == lax.axis_index("chan") % 2
    turn = jnp.where(solving, 0, 4)
    base = jnp.where((half == 1) & (j == 0), 1, 0)
    lanes = [pl.ds(pl.multiple_of((r + base + n) % 4 * T, T), T) for n in range(3)]
    loads = [
        pltpu.make_async_copy(vis.at[:, k, :, lanes[n]], vin.at[k, n], in_sem.at[k, n])
        for k in range(8)
        for n in range(3)
    ]
    stores = []
    for k in range(8):
        stores.append(pltpu.make_async_copy(chunk.at[k, :, 0:SPLIT], packed.at[k, :, 0:SPLIT], one_sem.at[k]))
        stores.append(
            pltpu.make_async_copy(chunk.at[k, :, SPLIT:], packed.at[(k + turn) % 8, :, SPLIT:], two_sem.at[k])
        )
    for load in loads:
        load.start()
    lane = lax.broadcasted_iota(jnp.int32, (32, T), 1)

    def run(place):
        for k in range(8):
            for load in loads[3 * k:3 * k + 3]:
                load.wait()

            def block(z, n):
                return vin[k, n, z]

            for z in range(2):
                if place == DIAGONAL:
                    chunk[k, z, 0:T, :] = block(z, 1)
                    third = block(z, 2)
                    turned = third.T[64:T]
                    chunk[k, z, T:T + 64, :] = jnp.where(r < 2, third[0:64], -turned if z else turned)
                    own = block(z, 0)
                    chunk[k, z, 192:224, :] = own[0:32]
                    chunk[k, z, 224:256, :] = jnp.where(lane < 32, pltpu.roll(own[96:T], 32, 1), own[32:64])
                    chunk[k, z, 256:, :] = jnp.where(lane[0:16] < 64, pltpu.roll(own[80:96], 64, 1), own[64:80])
                else:
                    chunk[k, z, 0:T, :] = block(z, 0)
                    second = block(z, 1)
                    if place == SOLVING:
                        chunk[k, z, T:2 * T, :] = second
                        chunk[k, z, 2 * T:, :] = block(z, 2)[0:THIRD]
                    else:
                        turned = second.T[THIRD:T]
                        chunk[k, z, T:2 * T - THIRD, :] = -turned if z else turned
                        chunk[k, z, 2 * T - THIRD:, :] = jnp.zeros((2 * THIRD, T), F32)
            stores[2 * k].start()
            stores[2 * k + 1].start()

    @pl.when(half == j)
    def _():
        run(DIAGONAL)

    @pl.when((half != j) & solving)
    def _():
        run(SOLVING)

    @pl.when((half != j) & jnp.logical_not(solving))
    def _():
        run(PASSING)

    for store in stores:
        store.wait()


def is_solver():
    return lax.axis_index("col") == lax.axis_index("chan") % 2


class Filler:
    def __init__(self, side, part_of, m_re, m_im, cc, halves, diag):
        self.refs = m_re, m_im, cc, halves, diag
        self.side, self.part_of = side, part_of

    def products(self, row, col, vr, vi):
        m_re, m_im = self.refs[:2]
        rs = pl.ds(pl.multiple_of(row * T, T), T)
        cs = pl.ds(pl.multiple_of(col * T, T), T)
        mr = m_re[rs, cs]
        mi = m_im[rs, cs]
        return vr * mr + vi * mi, vr * mi - vi * mr

    def put(self, row, col, parts):
        cc = self.refs[2]
        cs = pl.ds(pl.multiple_of(col * T, T), T)
        for n, part in enumerate(parts):
            cc[pl.ds(pl.multiple_of(n * 1024 + row * T, T), T), cs] = part.astype(BF16)

    def fill(self, row, col, vr, vi):
        self.put(row, col, self.products(row, col, vr, vi))
        self.put(col, row, self.products(col, row, vr.T, -vi.T))

    def own_block(self, a, z):
        row = lax.broadcasted_iota(jnp.int32, (T, T), 0)
        lane = lax.broadcasted_iota(jnp.int32, (T, T), 1)
        one = self.part_of(True, a, z, 192, 224)
        two = self.part_of(True, a, z, 224, 256)
        three = self.part_of(True, a, z, 256, ROWS)
        upper = jnp.concatenate([one, two, three, pltpu.roll(three, 64, 1), pltpu.roll(two, 96, 1)], 0)
        turned = upper.T
        return jnp.where((lane >> 5) >= (row >> 5), upper, -turned if z else turned)

    def inner(self):
        part_of, fill = self.part_of, self.fill
        halves, diag = self.refs[3:]
        jj = (lax.axis_index("col") + self.side) % 2
        eye = on_diagonal()

        def sources(r, _):
            a = 4 * jj + r
            parts = self.products(a, a, self.own_block(a, 0), self.own_block(a, 1))
            for n, part in enumerate(parts):
                diag[pl.ds(8 * n + a, 1), :] = jnp.sum(jnp.where(eye, part, 0.0), axis=0, keepdims=True)
            self.put(a, a, [jnp.where(eye, 0.0, part) for part in parts])
            fill(a, 4 * jj + (r + 1) % 4, part_of(True, a, 0, 0, T), part_of(True, a, 1, 0, T))
            for z in range(2):
                rs = pl.ds(pl.multiple_of((r // 2) * 64, 64), 64)
                halves[z, r % 2, rs, :] = part_of(True, a, z, T, T + 64)
            return 0

        lax.fori_loop(0, 4, sources, 0)

        def across(p, _):
            fill(4 * jj + p, 4 * jj + p + 2, halves[0, p], halves[1, p])
            return 0

        lax.fori_loop(0, 2, across, 0)

    def outer(self):
        part_of, fill = self.part_of, self.fill
        halves = self.refs[3]
        jj = (lax.axis_index("col") + self.side) % 2
        off = jnp.where(jj == 0, 1, 0)

        def sources(r, _):
            b = 4 * (1 - jj) + r
            fill(b, 4 * jj + (r + off) % 4, part_of(False, b, 0, 0, T), part_of(False, b, 1, 0, T))
            if self.side == 0:
                fill(b, 4 * jj + (r + off + 1) % 4, part_of(False, b, 0, T, 2 * T), part_of(False, b, 1, T, 2 * T))
            else:
                for z in range(2):
                    halves[z, 2 + (r + off + 1) % 4, THIRD:T, :] = part_of(False, b, z, T, 2 * T - THIRD)
            return 0

        lax.fori_loop(0, 4, sources, 0)


def on_diagonal():
    return lax.broadcasted_iota(jnp.int32, (T, T), 0) == lax.broadcasted_iota(jnp.int32, (T, T), 1)


def of_near(near):
    return lambda diagonal, a, z, lo, hi: near[a, z, lo:hi, :]


def of_far(far1, far2):
    def part_of(diagonal, a, z, lo, hi):
        parts = []
        if lo < SPLIT:
            parts.append(far1[a, z, lo:min(hi, SPLIT), :])
        if hi > SPLIT:
            start = max(lo, SPLIT)
            at = start - SPLIT + (0 if diagonal else ROWS - SPLIT)
            parts.append(far2[a % 4, z, at:at + hi - start, :])
        return parts[0] if len(parts) == 1 else jnp.concatenate(parts, 0)

    return part_of


def prepare(near, m_re, m_im, cc, diag, halves):
    @pl.when(is_solver())
    def _():
        eye = on_diagonal()

        def powers(a, _):
            rs = pl.ds(pl.multiple_of(a * T, T), T)
            out = pl.ds(pl.multiple_of(2048 + a * T, T), T)
            for t in range(8):
                lanes = slice(t * T, (t + 1) * T)
                mr = m_re[rs, lanes]
                mi = m_im[rs, lanes]
                cc[out, lanes] = (mr * mr + mi * mi).astype(BF16)
            lanes = pl.ds(pl.multiple_of(a * T, T), T)
            mr = m_re[rs, lanes]
            mi = m_im[rs, lanes]
            den = mr * mr + mi * mi
            diag[pl.ds(16 + a, 1), :] = jnp.sum(jnp.where(eye, den, 0.0), axis=0, keepdims=True)
            cc[out, lanes] = jnp.where(eye, 0.0, den).astype(BF16)
            return 0

        lax.fori_loop(0, 8, powers, 0)
        filler = Filler(0, of_near(near), m_re, m_im, cc, halves, diag)
        filler.inner()
        filler.outer()


def gain_solve(flags, part, part_diag, near, far1, far2, m_re, m_im, out, cc, halves, diag, sem):
    @pl.when(is_solver())
    def _():
        j = lax.axis_index("col")
        copies = []
        for n in range(2):
            mine = pl.ds(pl.multiple_of(n * 1024 + 512 * j, 512), 512)
            other = pl.ds(pl.multiple_of(n * 1024 + 512 * (1 - j), 512), 512)
            lanes = pl.ds(pl.multiple_of(512 * j, 512), 512)
            copies.append(pltpu.make_async_copy(part.at[mine], cc.at[mine], sem.at[n, 0]))
            copies.append(pltpu.make_async_copy(part.at[other, lanes], cc.at[other, lanes], sem.at[n, 1]))
        for copy in copies:
            copy.start()
        diag[...] = part_diag[...]
        solve(copies, flags, part, near, far1, far2, m_re, m_im, out, cc, halves, diag)

    @pl.when(jnp.logical_not(is_solver()))
    def _():
        out[...] = jnp.zeros_like(out)


def solve(copies, flags, part, near, far1, far2, m_re, m_im, out, cc, halves, diag):
    cp, j = lax.axis_index("row"), lax.axis_index("col")
    filler = Filler(1, of_far(far1, far2), m_re, m_im, cc, halves, diag)
    filler.inner()
    for copy in copies:
        copy.wait()
    filler.outer()
    near_off = jnp.where(j == 0, 1, 0)

    def thirds(r, _):
        a = 4 * (1 - j) + r
        for z in range(2):
            halves[z, 2 + r, 0:THIRD, :] = near[a, z, 2 * T:ROWS, :]
        filler.fill(a, 4 * j + (r + near_off + 2) % 4, halves[0, 2 + r], halves[1, 2 + r])
        return 0

    lax.fori_loop(0, 4, thirds, 0)
    w = flags[pl.ds(cp // 2, 1), :].astype(F32)

    def row_of(n):
        return jnp.concatenate([diag[8 * n + t:8 * n + t + 1, :] for t in range(8)], 1)

    d_re, d_im, d_den = row_of(0), row_of(1), row_of(2)
    sub = lax.broadcasted_iota(jnp.int32, (16, 1024), 0)

    def split(x):
        return x, x - x.astype(BF16).astype(F32)

    def stack(*rows):
        out = jnp.zeros((16, 1024), F32)
        for n, x in rows:
            out = jnp.where(sub == n, x, out)
        return out

    def one(step, carry):
        g_re, g_im = carry
        hr, hr_lo = split(w * g_re)
        hi, hi_lo = split(w * g_im)
        hd, hd_lo = split(w * (g_re * g_re + g_im * g_im))
        left = jnp.concatenate(
            [
                stack((0, hr), (1, hi), (3, hr_lo), (4, hi_lo)),
                stack((0, -hi), (1, hr), (3, -hi_lo), (4, hr_lo)),
            ],
            1,
        ).astype(BF16)
        powers = stack((2, hd), (5, hd_lo)).astype(BF16)
        sums = dot(left, cc[...], ((1,), (0,))) + dot(powers, part[2048:3072, :], ((1,), (0,)))
        num_re = sums[0:1] + sums[3:4] + (hr * d_re - hi * d_im)
        num_im = sums[1:2] + sums[4:5] + (hr * d_im + hi * d_re)
        den = sums[2:3] + sums[5:6] + hd * d_den
        scale = w / (den + 1.0 - w)
        n_re = num_re * scale
        n_im = num_im * scale
        odd = (step % 2) == 1
        return (
            jnp.where(odd, 0.5 * (n_re + g_re), n_re),
            jnp.where(odd, 0.5 * (n_im + g_im), n_im),
        )

    g_re, g_im = lax.fori_loop(0, ITERS, one, (w, jnp.zeros((1, 1024), F32)))
    for n in range(out.shape[0]):
        out[n, 0:1, :] = g_re
        out[n, 1:2, :] = g_im


def residual(vis, re_early, im_early, re_late, im_late, gall, res, gains, o, out_sem):
    i, j = lax.axis_index("row"), lax.axis_index("col")
    active = lax.axis_index("chan") % 2
    stores = [pltpu.make_async_copy(o.at[cp], res.at[:, cp], out_sem.at[cp]) for cp in range(8)]
    for n in range(8):
        for z in range(2):
            gains[z, n // 2, n % 2:n % 2 + 1, :] = gall[2 * n + active, z:z + 1, :]
    for cp in range(8):
        m_re, m_im = (re_early, im_early) if cp < 4 else (re_late, im_late)
        src = 2 * cp + active

        def lanes_of(z, t):
            return gall[src, z:z + 1, pl.ds(pl.multiple_of(t * T, T), T)]

        gpr = jnp.broadcast_to(lanes_of(0, i), (T, T)).T
        gpi = jnp.broadcast_to(lanes_of(1, i), (T, T)).T
        for q in range(4):
            lanes = slice(q * T, (q + 1) * T)
            gqr = lanes_of(0, 4 * j + q)
            gqi = lanes_of(1, 4 * j + q)
            mr = m_re[cp % 4, :, lanes]
            mi = m_im[cp % 4, :, lanes]
            ar = mr * gqr + mi * gqi
            ai = mi * gqr - mr * gqi
            o[cp, 0, :, lanes] = vis[0, cp, :, lanes] - (gpr * ar - gpi * ai)
            o[cp, 1, :, lanes] = vis[1, cp, :, lanes] - (gpr * ai + gpi * ar)
        stores[cp].start()
    for store in stores:
        store.wait()


SMEM = pl.BlockSpec(memory_space=pltpu.SMEM)
VMEM = pl.BlockSpec(memory_space=pltpu.VMEM)
ANY = pl.BlockSpec(memory_space=pl.ANY)


def vmem(mib):
    return pltpu.CompilerParams(vmem_limit_bytes=mib << 20)


def shape(*dims):
    return jax.ShapeDtypeStruct(dims, F32)


def body(rows, cols, chans, visibilities, stations, pixels, flux, freqs, flags):
    vis = visibilities.reshape(2, 8, T, 512)
    st = stations.reshape(2, 8, T)
    pix = pixels.reshape(8, T)
    fx = flux.reshape(8, 8, T)

    with jax.named_scope("pack"):
        packed = pl.pallas_call(
            pack,
            out_shape=shape(8, 2, ROWS, T),
            in_specs=[ANY],
            out_specs=ANY,
            scratch_shapes=[
                pltpu.VMEM((8, 3, 2, T, T), F32),
                pltpu.VMEM((8, 2, ROWS, T), F32),
                pltpu.SemaphoreType.DMA((8, 3)),
                pltpu.SemaphoreType.DMA((8,)),
                pltpu.SemaphoreType.DMA((8,)),
            ],
            compiler_params=vmem(60),
            cost_estimate=pl.CostEstimate(flops=1 << 20, bytes_accessed=7 << 20, transcendentals=0),
        )(vis)
    with jax.named_scope("to_the_rows"):
        near = lax.all_to_all(packed, "row", 0, 0, tiled=True)

    with jax.named_scope("own_model"):
        m_re, m_im = pl.pallas_call(
            own_model,
            out_shape=(shape(1024, 1024),) * 2,
            in_specs=[SMEM, VMEM, VMEM, VMEM],
            out_specs=(ANY,) * 2,
            scratch_shapes=[
                pltpu.VMEM((1024, T), F32),
                pltpu.VMEM((1024, T), F32),
                pltpu.VMEM((1024, 2048), BF16),
                pltpu.VMEM((1024, 3072), BF16),
                pltpu.VMEM((2, 1024, 1024), F32),
                pltpu.SemaphoreType.DMA((2, 4)),
            ],
            compiler_params=vmem(60),
            cost_estimate=pl.CostEstimate(flops=8 << 30, bytes_accessed=8 << 20, transcendentals=8 << 20),
        )(freqs, st, pix, fx)
    def block(first):
        return pl.pallas_call(
            functools.partial(block_model, first),
            out_shape=(shape(4, T, 512),) * 2,
            in_specs=[SMEM, VMEM, VMEM, VMEM],
            out_specs=(ANY,) * 2,
            scratch_shapes=[
                pltpu.VMEM((T, T), F32),
                pltpu.VMEM((T, T), F32),
                pltpu.VMEM((1024, T), F32),
                pltpu.VMEM((1024, T), F32),
                pltpu.VMEM((256, 3072), BF16),
                pltpu.VMEM((2048, 512), BF16),
                pltpu.VMEM((2, 4, T, 512), F32),
                pltpu.SemaphoreType.DMA((2, 2)),
            ],
            compiler_params=vmem(14),
            cost_estimate=pl.CostEstimate(flops=4 << 30, bytes_accessed=2 << 20, transcendentals=4 << 20),
        )(freqs, st, pix, fx)

    with jax.named_scope("to_the_active_column"):
        near, m_re, m_im, *early = lax.optimization_barrier((near, m_re, m_im, *block(0)))
        mine = 4 * lax.axis_index("col")
        pieces = [
            near[:, :, 0:SPLIT],
            jnp.concatenate(
                [
                    lax.dynamic_slice_in_dim(near, mine, 4)[:, :, SPLIT:ROWS],
                    lax.dynamic_slice_in_dim(near, 4 - mine, 4)[:, :, SPLIT:2 * T - THIRD],
                ],
                2,
            ),
        ]
        far = []
        for piece, turn in zip(pieces, (0, rows // 2)):
            pairs = []
            for z in range(chans):
                to = z % 2
                for r in range(rows):
                    src = (r * cols + 1 - to) * chans + z
                    dst = ((r + turn) % rows * cols + to) * chans + z
                    pairs.append((src, dst))
            far.append(lax.ppermute(piece, ("row", "col", "chan"), pairs))

    with jax.named_scope("block_model"):
        late = block(2)
    with jax.named_scope("prepare"):
        part, part_diag = pl.pallas_call(
            prepare,
            out_shape=(jax.ShapeDtypeStruct((3072, 1024), BF16), shape(24, T)),
            in_specs=[VMEM] * 3,
            out_specs=(VMEM, VMEM),
            scratch_shapes=[pltpu.VMEM((2, 2, T, T), F32)],
            compiler_params=vmem(18),
            cost_estimate=pl.CostEstimate(flops=16 << 20, bytes_accessed=16 << 20, transcendentals=0),
        )(near, m_re, m_im)
    far[0], far[1], part, *late = lax.optimization_barrier((far[0], far[1], part, *late))

    with jax.named_scope("gain_solve"):
        g = pl.pallas_call(
            gain_solve,
            out_shape=shape(rows * cols, 2, 1024),
            in_specs=[VMEM] * 8,
            out_specs=VMEM,
            scratch_shapes=[
                pltpu.VMEM((2048, 1024), BF16),
                pltpu.VMEM((2, 6, T, T), F32),
                pltpu.VMEM((24, T), F32),
                pltpu.SemaphoreType.DMA((2, 2)),
            ],
            compiler_params=vmem(27),
            cost_estimate=pl.CostEstimate(flops=800 << 20, bytes_accessed=14 << 20, transcendentals=0),
        )(flags, part, part_diag, near, *far, m_re, m_im)

    with jax.named_scope("gather_gains"):
        gall = lax.all_to_all(g, ("row", "col"), 0, 0, tiled=True)

    with jax.named_scope("residual"):
        res, gains = pl.pallas_call(
            residual,
            out_shape=(shape(2, 8, T, 512), shape(2, 4, 2, 1024)),
            in_specs=[VMEM] * 6,
            out_specs=(ANY, VMEM),
            scratch_shapes=[pltpu.VMEM((8, 2, T, 512), F32), pltpu.SemaphoreType.DMA((8,))],
            compiler_params=vmem(14),
            cost_estimate=pl.CostEstimate(flops=32 << 20, bytes_accessed=12 << 20, transcendentals=0),
        )(vis, *early, *late, gall)
    return gains, res.reshape(2, 4, 2, T, 512)


def solution(mesh):
    in_specs = (
        P(None, "chan", None, "row", "col"),
        P(None, "chan"),
        P("chan"),
        P("chan", None, None),
        P("chan"),
        P("chan", None),
    )
    out_specs = (P(None, "chan", None, None), P(None, "chan", None, "row", "col"))
    run = functools.partial(body, mesh.shape["row"], mesh.shape["col"], mesh.shape["chan"])
    return jax.shard_map(run, mesh=mesh, in_specs=in_specs, out_specs=out_specs, check_vma=False)
```
